32 devices in a mesh: slab: 4 (over z), brick: 8 (over y, x, core).
Axes of the slice: x: 2, y: 2, z: 4, core: 2. Of those that a mesh axis runs over, the one named last changes fastest.
Arguments:
- pressure: float32 [32, 64, 256], P('slab', 'brick'), may hold values from -6 to 6
- previous: float32 [32, 64, 256], P('slab', 'brick'), may hold values from -6 to 6
- radius: float32 [2048, 128], P(('slab', 'brick')), may hold values from 0.8 to 1.25
- velocity: float32 [2048, 128], P(('slab', 'brick')), may hold values from -1 to 1
- positions: float32 [3, 2048, 128], P(None, ('slab', 'brick')), may hold values from 0 to 1
- occupancy: int32 [2048], P(('slab', 'brick')), may hold values from 1 to 128
- anchors: int32 [3, 3, 2048], P(None, None, ('slab', 'brick')), may hold values from 0 to 224, as said below
- migrations: int32 [3, 2048], P(None, ('slab', 'brick')), may hold values from 0 to 63, as said below
- crossings: int32 [3, 32], P(None, ('slab', 'brick')), may hold values from 0 to 32, as said below
Outputs:
- final_pressure: float32 [32, 64, 256], P('slab', 'brick')
- final_radius: float32 [2048, 128], P(('slab', 'brick'))
- final_velocity: float32 [2048, 128], P(('slab', 'brick'))
The draws below stay inside these ranges and needn't reach their ends.
Inputs may be any that keep to these rules, and one draw needn't show every extreme that they name: anchors[s, 0] lies in 0 to 7, anchors[s, 1] in 0 to 7, anchors[s, 2] in 0 to 224. `migrations`: for each step and owner the 64 listed slots are distinct local slots. `crossings`: the entry of the last brick of each slab is 0; in every step some border carries exactly 32 bins.
All inputs are finite; a program needn't handle non-finite values.
Results may differ from the reference program's by a relative error of at most 0.0003.
Values sent between devices are 32-bit elements; how exact they have to be, the bound alone decides.
A program may use at most 64 MiB of HBM per device.

```python
import math
import jax
import jax.numpy as jnp
from jax import lax

CX = 8
CY = 8
CZ = 256
BINS_DEV = 64
MOST = 32
BIN = 128
PZ = 32
STEPS = 3
SLABS = 4
BRICKS = 8
OWNERS = 32
NX = 32
NY = 64
NZ = 256
BINS_ALL = 2048


def draw_anchors(key, part):
    key = jax.random.fold_in(key, 11)
    key_set = jax.random.split(key, 3)
    along_x = jax.random.randint(key_set[0], (STEPS, 1, BINS_ALL), 0, CX)
    along_y = jax.random.randint(key_set[1], (STEPS, 1, BINS_ALL), 0, CY)
    along_z = jax.random.randint(key_set[2], (STEPS, 1, BINS_ALL), 0, CZ - PZ + 1)
    return jnp.concatenate([along_x, along_y, along_z], axis=1).astype(jnp.int32)


def draw_migrations(key, part):
    key = jax.random.fold_in(key, 23)
    key_set = jax.random.split(key, STEPS * OWNERS)

    def draw_list(subkey):
        return jax.random.permutation(subkey, BINS_DEV)[:2 * MOST].astype(jnp.int32)
    return jax.vmap(draw_list)(key_set).reshape(STEPS, OWNERS * 2 * MOST)


def draw_crossings(key, part):
    key = jax.random.fold_in(key, 37)
    key_set = jax.random.split(key, 2)
    row_count = OWNERS // BRICKS
    crossing = jax.random.randint(key_set[0], (STEPS, row_count, BRICKS), MOST // 4, MOST + 1)
    chosen = jax.random.randint(key_set[1], (STEPS, row_count, 1), 0, BRICKS - 1)
    bricks = jnp.arange(BRICKS)[None, None, :]
    crossing = jnp.where(bricks == chosen, MOST, crossing)
    crossing = jnp.where(bricks == BRICKS - 1, 0, crossing)
    return crossing.reshape(STEPS, OWNERS).astype(jnp.int32)


def with_ends(array, rng, smallest, top_value):
    spot = [jax.random.randint(jax.random.fold_in(rng, axis), (), 0, length) for axis, length in enumerate(array.shape)]
    widest = array.shape.index(max(array.shape))
    next_to = spot[:widest] + [(spot[widest] + 1) % array.shape[widest]] + spot[widest + 1:]
    return array.at[tuple(spot)].set(smallest).at[tuple(next_to)].set(top_value)


def level_of(rng, dims, cuts, low, largest):
    factor_of = 1.0
    for axis_at, shards_of in cuts:
        heights = jax.random.uniform(jax.random.fold_in(jax.random.fold_in(rng, 6), axis_at), (shards_of,), jnp.float32, low / len(cuts), largest / len(cuts))
        factor_of = factor_of * jnp.repeat(jnp.exp(heights), dims[axis_at] // shards_of).reshape((-1,) + (1,) * (len(dims) - 1 - axis_at))
    return factor_of


def bell_draw(own_key, shape, deviation, most, pieces=(), kind=jnp.bfloat16):
    result = deviation * jax.random.normal(own_key, shape, jnp.float32)
    if pieces:
        result = result * level_of(own_key, shape, pieces, -0.22, 0.18)
    return jnp.clip(result, -most, most).astype(kind)


def setup_inputs(seed: int = 0) -> dict:
    seeds = jax.random.split(jax.random.key(seed), 10)
    return {
        "pressure": bell_draw(seeds[0], (NX, NY, NZ), 1.0, 6.0, ((0, 4), (1, 8)), jnp.float32),
        "previous": bell_draw(seeds[1], (NX, NY, NZ), 1.0, 6.0, ((0, 4), (1, 8)), jnp.float32),
        "radius": jnp.clip(jnp.exp(math.log(1.25) - 0.4462871 * jax.random.uniform(seeds[2], (BINS_ALL, BIN), jnp.float32) ** level_of(seeds[2], (BINS_ALL, BIN), ((0, 32),), -0.2, 0.2)), 0.8, 1.25),
        "velocity": bell_draw(seeds[3], (BINS_ALL, BIN), 0.2, 1.0, ((0, 32),), jnp.float32),
        "positions": jnp.clip(1.0 * jax.random.uniform(seeds[4], (3, BINS_ALL, BIN), jnp.float32) ** level_of(seeds[4], (3, BINS_ALL, BIN), ((1, 32),), -0.2, 0.2), 0.0, 1.0),
        "occupancy": with_ends(jax.random.randint(seeds[5], (BINS_ALL,), 1, BIN + 1), jax.random.fold_in(seeds[5], 1), 1, BIN).astype(jnp.int32),
        "anchors": draw_anchors(jax.random.fold_in(seeds[9], 71), 0),
        "migrations": draw_migrations(jax.random.fold_in(seeds[9], 71), 0),
        "crossings": draw_crossings(jax.random.fold_in(seeds[9], 71), 0),
    }


courant_square = 0.25
source_gain = 0.05
kernel_width = 2.25
gas_pressure = 1.2
surface_tension = 0.1
viscosity = 0.02
polytropic = 1.4
sound_speed = 20.0
drive_gain = 0.5
time_step = 0.05
four_pi = 12.566370614359172


def factor(coordinate, extent, stretch):
    places = jnp.arange(extent).astype(jnp.float32)
    weight = jnp.exp(-(coordinate[..., None] * stretch - places) ** 2 / (2.0 * kernel_width))
    return weight / jnp.sum(weight, axis=-1, keepdims=True)


def smear_kernel(positions):
    along_x = factor(positions[0], 2, 1.0)
    along_y = factor(positions[1], 2, 1.0)
    along_z = factor(positions[2], PZ, PZ - 1.0)
    joined = along_x[..., :, None, None] * along_y[..., None, :, None] * along_z[..., None, None, :]
    return joined.reshape(joined.shape[:-3] + (4 * PZ,))


def wall_accel(radius, velocity, outside):
    gas_term = gas_pressure * jnp.exp(-3.0 * polytropic * jnp.log(radius))
    wall_term = gas_term - 2.0 * surface_tension / radius - 4.0 * viscosity * velocity / radius
    ambient = 1.0 + drive_gain * outside
    mach_number = velocity / sound_speed
    driving = (1.0 + mach_number) * (wall_term - ambient) - 1.5 * (1.0 - mach_number / 3.0) * velocity * velocity
    return driving / ((1.0 - mach_number) * radius)


def bubble_block(bubbles, patches, occupancy):
    kernel = smear_kernel(bubbles[2:])
    outside = jnp.einsum("gnc,gc->gn", kernel, patches, precision=lax.Precision.HIGHEST)
    radius, velocity = bubbles[0], bubbles[1]
    first_accel = wall_accel(radius, velocity, outside)
    mid_radius = radius + 0.5 * time_step * velocity
    mid_velocity = velocity + 0.5 * time_step * first_accel
    second_accel = wall_accel(mid_radius, mid_velocity, outside)
    new_radius = radius + time_step * mid_velocity
    new_velocity = velocity + time_step * second_accel
    volume = four_pi * (2.0 * mid_radius * mid_velocity * mid_velocity + mid_radius * mid_radius * second_accel)
    living = jnp.arange(BIN)[None, :] < occupancy[:, None]
    volume = jnp.where(living, volume, jnp.zeros_like(volume))
    deposit = jnp.einsum("gn,gnc->gc", volume, kernel, precision=lax.Precision.HIGHEST)
    return new_radius, new_velocity, deposit


def read_patch(padded, corner_x, corner_y, corner_z):
    return lax.dynamic_slice(padded, (corner_x + 1, corner_y + 1, corner_z), (2, 2, PZ)).reshape(4 * PZ)


def deposit_indices(corner_x, corner_y, corner_z):
    cell_index = jnp.arange(4 * PZ)
    index_x = corner_x[:, None] + cell_index[None, :] // (2 * PZ)
    index_y = corner_y[:, None] + (cell_index[None, :] // PZ) % 2
    index_z = corner_z[:, None] + cell_index[None, :] % PZ
    return index_x, index_y, index_z


def advance(pressure, previous, padded, source):
    neighbours = padded[2:, 1:-1] + padded[:-2, 1:-1] + padded[1:-1, 2:] + padded[1:-1, :-2]
    depth_padded = jnp.pad(pressure, ((0, 0), (0, 0), (1, 1)))
    neighbours = neighbours + depth_padded[:, :, 2:] + depth_padded[:, :, :-2]
    laplace = neighbours - 6.0 * pressure
    return 2.0 * pressure - previous + courant_square * laplace + source_gain * source


def place(bubbles, occupancy, slot_list, incoming, incoming_occupancy, number):
    living = jnp.arange(slot_list.shape[0]) < number
    current = bubbles[:, slot_list]
    bubbles = bubbles.at[:, slot_list].set(jnp.where(living[None, :, None], incoming, current))
    occupancy = occupancy.at[slot_list].set(jnp.where(living, incoming_occupancy, occupancy[slot_list]))
    return bubbles, occupancy


def neighbour(values, offset, device_axis):
    layout = values.shape
    reshaped = values.reshape(layout[:device_axis] + (SLABS, BRICKS) + layout[device_axis + 1:])
    rolled = jnp.roll(reshaped, offset, axis=device_axis + 1)
    bricks = jnp.arange(BRICKS) - offset
    inside = (bricks >= 0) & (bricks < BRICKS)
    inside = inside.reshape((1,) * (device_axis + 1) + (BRICKS,) + (1,) * (len(layout) - device_axis - 1))
    return jnp.where(inside, rolled, jnp.zeros_like(rolled)).reshape(layout)


def migrate_all(bubbles, occupancy, slot_row, crossing):
    grouped = bubbles.reshape(5, OWNERS, BINS_DEV, BIN)
    owned = occupancy.reshape(OWNERS, BINS_DEV)
    slot_table = slot_row.reshape(OWNERS, 2 * MOST)
    left_slots = slot_table[:, :MOST]
    right_slots = slot_table[:, MOST:]
    pick = jax.vmap(lambda block, chosen: block[:, chosen], in_axes=(1, 0), out_axes=1)
    pick_owned = jax.vmap(lambda block, chosen: block[chosen])
    from_below = neighbour(pick(grouped, right_slots), 1, 1)
    from_above = neighbour(pick(grouped, left_slots), -1, 1)
    owned_below = neighbour(pick_owned(owned, right_slots), 1, 0)
    owned_above = neighbour(pick_owned(owned, left_slots), -1, 0)
    number_below = neighbour(crossing, 1, 0)
    placing = jax.vmap(place, in_axes=(1, 0, 0, 1, 0, 0), out_axes=(1, 0))
    grouped, owned = placing(grouped, owned, right_slots, from_above, owned_above, crossing)
    grouped, owned = placing(grouped, owned, left_slots, from_below, owned_below, number_below)
    return grouped.reshape(5, BINS_ALL, BIN), owned.reshape(BINS_ALL)


def reference(pressure, previous, radius, velocity, positions, occupancy, anchors, migrations, crossings):
    bubbles = jnp.concatenate([radius[None], velocity[None], positions], axis=0)
    owners = jnp.arange(BINS_ALL) // BINS_DEV
    offset_x = ((owners // BRICKS) * CX).astype(jnp.int32)
    offset_y = ((owners % BRICKS) * CY).astype(jnp.int32)
    for step_index in range(STEPS):
        bubbles, occupancy = migrate_all(bubbles, occupancy, migrations[step_index], crossings[step_index])
        padded = jnp.pad(pressure, ((1, 1), (1, 1), (0, 0)))
        corner_x = anchors[step_index, 0] + offset_x
        corner_y = anchors[step_index, 1] + offset_y
        corner_z = anchors[step_index, 2]
        patches = jax.vmap(read_patch, in_axes=(None, 0, 0, 0))(padded, corner_x, corner_y, corner_z)
        blocks = (bubbles.reshape(5, OWNERS, BINS_DEV, BIN).transpose(1, 0, 2, 3),
                  patches.reshape(OWNERS, BINS_DEV, 4 * PZ),
                  occupancy.reshape(OWNERS, BINS_DEV))
        new_radius, new_velocity, deposit = lax.map(lambda block: bubble_block(block[0], block[1], block[2]), blocks)
        index_x, index_y, index_z = deposit_indices(corner_x, corner_y, corner_z)
        collected = jnp.zeros((NX + 1, NY + 1, NZ), jnp.float32)
        collected = collected.at[index_x, index_y, index_z].add(deposit.reshape(BINS_ALL, 4 * PZ))
        source = collected[:NX, :NY]
        new_pressure = advance(pressure, previous, padded, source)
        previous, pressure = pressure, new_pressure
        bubbles = jnp.concatenate([new_radius.reshape(1, BINS_ALL, BIN), new_velocity.reshape(1, BINS_ALL, BIN), bubbles[2:]], axis=0)
    return pressure, bubbles[0], bubbles[1]
```

```python
import functools

import jax
import jax.numpy as jnp
from jax import lax
from jax.experimental import pallas as pl
from jax.experimental.pallas import tpu as pltpu
from jax.sharding import PartitionSpec as P

BIN = 128
PZ = 32
STEPS = 3

courant_square = 0.25
source_gain = 0.05
kernel_width = 2.25
gas_pressure = 1.2
surface_tension = 0.1
viscosity = 0.02
polytropic = 1.4
sound_speed = 20.0
drive_gain = 0.5
time_step = 0.05
four_pi = 12.566370614359172
root = (1.4426950408889634 / (2.0 * kernel_width)) ** 0.5

MESH = pl.DeviceIdType.MESH
F32 = jnp.float32
BF16 = jnp.bfloat16

X_HIGH, X_LOW, Y_HIGH, Y_LOW, CORNER = range(5)
DEP_X, DEP_Y, DEP_CORNER = range(5, 8)
FIX_UP, FIX_DOWN, RV_UP, RV_DOWN, COUNT = range(8, 13)
OFFSETS = (
    (-1, 0), (1, 0), (0, -1), (0, 1), (-1, -1),
    (1, 0), (0, 1), (1, 1),
    (0, 1), (0, -1), (0, 1), (0, -1), (0, 1),
)
KINDS = len(OFFSETS)


def pieces(value, count):
    found = []
    for _ in range(count - 1):
        piece = value.astype(BF16)
        found.append(piece)
        value = value - piece.astype(F32)
    found.append(value.astype(BF16))
    return found


def picked(one_hot, value, count):
    total = None
    for piece in pieces(value, count):
        term = jnp.dot(one_hot, piece, preferred_element_type=F32)
        total = term if total is None else total + term
    return total


def wall_accel(radius, velocity, outside):
    gas_term = gas_pressure * jnp.exp(-3.0 * polytropic * jnp.log(radius))
    inverse = 1.0 / radius
    wall_term = gas_term - (2.0 * surface_tension + 4.0 * viscosity * velocity) * inverse
    ambient = 1.0 + drive_gain * outside
    mach_number = velocity * (1.0 / sound_speed)
    driving = (1.0 + mach_number) * (wall_term - ambient) - 1.5 * (
        1.0 - mach_number * (1.0 / 3.0)
    ) * velocity * velocity
    return driving / ((1.0 - mach_number) * radius)


def iota(shape, dim):
    return lax.broadcasted_iota(jnp.int32, shape, dim)


def pair_factor(fraction):
    low = jnp.exp2(-jnp.square(fraction * root))
    high = jnp.exp2(-jnp.square((fraction - 1.0) * root))
    total = 1.0 / (low + high)
    return low * total, high * total


def kernel(
    slabs, bricks,
    pressure, previous, radius, velocity, positions, occupancy, anchors, migrations, crossings,
    out_pressure, out_radius, out_velocity,
    halo, edge, dep_in, dep_out, fix_in, fix_out, fix, rv_in, rv_out, rv, counts, field,
    rows, placed, fresh, corner_z, take, put, turn, send_sem, recv_sem,
):
    cells_x, cells_y, depth = pressure.shape
    bins = radius.shape[0]
    most = bins // 2
    own = cells_x * cells_y
    slab, brick = lax.axis_index("slab"), lax.axis_index("brick")

    def inside(dx, dy):
        a, b = slab + dx, brick + dy
        return (a >= 0) & (a < slabs) & (b >= 0) & (b < bricks)

    barrier = pltpu.get_barrier_semaphore()
    near = ((1, 0), (-1, 0), (0, 1), (0, -1), (1, 1), (-1, -1))
    expected = jnp.int32(0)
    for dx, dy in near:
        expected = expected + inside(dx, dy).astype(jnp.int32)

        @pl.when(inside(dx, dy))
        def _():
            pl.semaphore_signal(
                barrier, inc=1, device_id=(slab + dx, brick + dy), device_id_type=MESH
            )

    pending = []

    def copy(kind, step, source, target):
        dx, dy = OFFSETS[kind]
        return pltpu.make_async_remote_copy(
            src_ref=source,
            dst_ref=target,
            send_sem=send_sem.at[step, kind],
            recv_sem=recv_sem.at[step, kind],
            device_id=(slab + dx, brick + dy),
            device_id_type=MESH,
        )

    def send(kind, step, source, target):
        made = copy(kind, step, source, target)
        there = inside(*OFFSETS[kind])

        @pl.when(there)
        def _():
            made.start()

        pending.append((there, made))

    def arrive(kind, step, target):
        dx, dy = OFFSETS[kind]

        @pl.when(inside(-dx, -dy))
        def _():
            copy(kind, step, target, target).wait_recv()

    eye = iota((bins, bins), 0) == iota((bins, bins), 1)

    def column(row):
        return jnp.sum(jnp.where(eye, jnp.broadcast_to(row, (bins, bins)), 0.0), axis=1, keepdims=True)

    slot_row = iota((1, bins), 1).astype(F32)
    slot_column = iota((bins, 1), 0).astype(F32)
    list_rows = [migrations[s : s + 1, :].astype(F32) for s in range(STEPS)]
    list_columns = [column(row) for row in list_rows]

    def turn_of(s):
        before = slot_row if s == 0 else list_rows[s - 1]
        after = slot_column if s == STEPS else list_columns[s]
        return (after == before).astype(F32).astype(BF16)

    def send_fix(s, value):
        fix_out[s] = value
        send(FIX_UP, s, fix_out.at[s, pl.ds(most, most)], fix_in.at[s, 0])
        send(FIX_DOWN, s, fix_out.at[s, pl.ds(0, most)], fix_in.at[s, 1])

    def send_rv(s, value):
        rv_out[s] = value
        send(RV_UP, s, rv_out.at[s, pl.ds(most, most)], rv_in.at[s, 0])
        send(RV_DOWN, s, rv_out.at[s, pl.ds(0, most)], rv_in.at[s, 1])

    def send_halo(s, block):
        edge[s, 0] = jnp.concatenate([block[x, 0:1, :] for x in range(cells_x)], axis=0)
        edge[s, 1] = jnp.concatenate(
            [block[x, cells_y - 1 : cells_y, :] for x in range(cells_x)], axis=0
        )
        send(X_HIGH, s, block.at[0], halo.at[s, X_HIGH])
        send(X_LOW, s, block.at[cells_x - 1], halo.at[s, X_LOW])
        send(Y_HIGH, s, edge.at[s, 0], halo.at[s, Y_HIGH])
        send(Y_LOW, s, edge.at[s, 1], halo.at[s, Y_LOW])
        send(CORNER, s, block.at[0], halo.at[s, CORNER])

    listed = iota((most, 1), 0)

    def merged(kind_up, kind_down, s, arrived, sent):
        arrive(kind_up, s, arrived.at[s, 0])
        arrive(kind_down, s, arrived.at[s, 1])
        width = sent.shape[2]
        from_below = jnp.broadcast_to(listed < counts[1, s : s + 1, 0:1], (most, width))
        from_above = jnp.broadcast_to(listed < counts[0, s : s + 1, 0:1], (most, width))
        return jnp.concatenate(
            [
                jnp.where(from_below, arrived[s, 0], sent[s, 0:most, :]),
                jnp.where(from_above, arrived[s, 1], sent[s, most:bins, :]),
            ],
            axis=0,
        )

    count_row = iota((8, 128), 0)
    my_counts = jnp.zeros((8, 128), jnp.int32)
    for s in range(STEPS):
        my_counts = jnp.where(count_row == s, crossings[s, 0], my_counts)
    counts[0] = my_counts

    for kind in range(5):
        dx, dy = OFFSETS[kind]

        @pl.when(jnp.logical_not(inside(-dx, -dy)))
        def _():
            for s in range(STEPS):
                halo[s, kind] = jnp.zeros((cells_y, depth), F32)

    for kind in (DEP_X, DEP_Y, DEP_CORNER):
        dx, dy = OFFSETS[kind]

        @pl.when(jnp.logical_not(inside(-dx, -dy)))
        def _():
            for s in range(STEPS):
                dep_in[s, kind - 5] = jnp.zeros((cells_y, depth), F32)

    @pl.when(brick == 0)
    def _():
        counts[1] = jnp.zeros((8, 128), jnp.int32)

    alive = jnp.broadcast_to(column(occupancy[...].astype(F32)), (bins, BIN))
    first = jnp.concatenate(
        [radius[...], velocity[...], positions[0], positions[1], positions[2], alive], axis=1
    )
    first = picked(turn_of(0), first, 3)

    pl.semaphore_wait(barrier, expected)
    counts_copy = copy(COUNT, 0, counts.at[0], counts.at[1])
    there = inside(*OFFSETS[COUNT])

    @pl.when(there)
    def _():
        counts_copy.start()

    pending.append((there, counts_copy))
    send_fix(0, first[:, 2 * BIN :])
    send_halo(0, pressure)
    send_rv(0, first[:, : 2 * BIN])

    for s in range(STEPS):
        chosen = list_columns[s] == slot_row
        corner = [
            jnp.sum(
                jnp.where(chosen, anchors[s, d : d + 1, :].astype(F32), 0.0), axis=1, keepdims=True
            )
            for d in range(3)
        ]
        corner_z[s] = jnp.broadcast_to(corner[2].astype(jnp.int32), (bins, BIN))
        turn[s + 1] = turn_of(s + 1)

        def cell_of(x, y):
            return jnp.where(y < cells_y, x * cells_y + y, own + cells_y + x)

        mine = iota((bins, 4 * bins), 1) % bins == iota((bins, 4 * bins), 0)
        x_row, y_row = [
            jnp.sum(jnp.where(mine, corner[d], 0.0), axis=0, keepdims=True).astype(jnp.int32)
            for d in range(2)
        ]
        which = iota((1, 4 * bins), 1) // bins
        cells = cell_of(x_row + which // 2, y_row + which % 2)
        put[s] = (iota((128, 4 * bins), 0) == cells).astype(F32).astype(BF16)
        x_column, y_column = corner[0].astype(jnp.int32), corner[1].astype(jnp.int32)
        cells = jnp.concatenate(
            [cell_of(x_column + c // 2, y_column + c % 2) for c in range(4)], axis=0
        )
        take[s] = (iota((4 * bins, 128), 1) == cells).astype(F32).astype(BF16)

    arrive(COUNT, 0, counts.at[1])
    fix[0] = merged(FIX_UP, FIX_DOWN, 0, fix_in, fix_out)
    send_fix(1, picked(turn[1], fix[0], 3))

    lane = iota((8, 128), 1)
    for s in range(STEPS):
        now = pressure if s == 0 else field.at[s - 1]
        before = previous if s == 0 else (pressure if s == 1 else field.at[s - 2])
        for kind in (X_HIGH, Y_HIGH, CORNER):
            arrive(kind, s, halo.at[s, kind])
        corner_row = jnp.where(iota((cells_y, depth), 0) == 0, halo[s, CORNER], 0.0)
        cells = jnp.concatenate(
            [
                now[...].reshape(own, depth),
                halo[s, X_HIGH],
                halo[s, Y_HIGH],
                corner_row,
                jnp.zeros((128 - own - 3 * cells_y, depth), F32),
            ],
            axis=0,
        )
        rows[...] = picked(take[s], cells, 2)
        rv[...] = merged(RV_UP, RV_DOWN, s, rv_in, rv_out)

        def group(index, carry):
            at = pl.ds(pl.multiple_of(index * 8, 8), 8)
            start = corner_z[s, at, :]
            z = start + lane % PZ
            high = z >= 128
            z = z % 128
            patch = None
            for c in range(4):
                those = pl.ds(pl.multiple_of(c * bins + index * 8, 8), 8)
                low_part = jnp.take_along_axis(
                    rows[those, 0:128], z, axis=1, mode="promise_in_bounds"
                )
                high_part = jnp.take_along_axis(
                    rows[those, 128:256], z, axis=1, mode="promise_in_bounds"
                )
                both = jnp.where(high, high_part, low_part)
                patch = both if c == 0 else jnp.where(lane // PZ == c, both, patch)
            x_pair = pair_factor(fix[s, at, 0:BIN])
            y_pair = pair_factor(fix[s, at, BIN : 2 * BIN])
            scaled = fix[s, at, 2 * BIN : 3 * BIN] * ((PZ - 1.0) * root)
            live = fix[s, at, 3 * BIN : 4 * BIN]
            weight = [jnp.exp2(-jnp.square(scaled - k * root)) for k in range(PZ)]
            total = weight[0]
            for k in range(1, PZ):
                total = total + weight[k]
            norm = 1.0 / total
            planar = [x_pair[c // 2] * (y_pair[c % 2] * norm) for c in range(4)]
            outside = None
            for c in range(4):
                part = None
                for k in range(PZ):
                    spot = c * PZ + k
                    term = weight[k] * patch[:, spot : spot + 1]
                    part = term if part is None else part + term
                part = part * planar[c]
                outside = part if outside is None else outside + part
            r, v = rv[at, 0:BIN], rv[at, BIN : 2 * BIN]
            first_accel = wall_accel(r, v, outside)
            mid_r = r + 0.5 * time_step * v
            mid_v = v + 0.5 * time_step * first_accel
            second_accel = wall_accel(mid_r, mid_v, outside)
            fresh[at, 0:BIN] = r + time_step * mid_v
            fresh[at, BIN : 2 * BIN] = v + time_step * second_accel
            volume = four_pi * (2.0 * mid_r * mid_v * mid_v + mid_r * mid_r * second_accel)
            volume = jnp.where(lane.astype(F32) < live, volume, 0.0)
            given = jnp.zeros((8, 128), F32)
            for c in range(4):
                share = planar[c] * volume
                for k in range(PZ):
                    amount = jnp.sum(share * weight[k], axis=1, keepdims=True)
                    given = jnp.where(lane == c * PZ + k, amount, given)
            for half in range(depth // 128):
                away = lane + 128 * half - start
                valid = (away >= 0) & (away < PZ)
                away = jnp.clip(away, 0, PZ - 1)
                for c in range(4):
                    those = pl.ds(pl.multiple_of(c * bins + index * 8, 8), 8)
                    found = jnp.take_along_axis(
                        given, away + c * PZ, axis=1, mode="promise_in_bounds"
                    )
                    placed[those, 128 * half : 128 * (half + 1)] = jnp.where(valid, found, 0.0)
            return carry

        lax.fori_loop(0, bins // 8, group, 0)

        collected = picked(put[s], placed[...], 2)
        dep_out[s] = collected[own : own + 3 * cells_y, :]
        for part, kind in enumerate((DEP_X, DEP_Y, DEP_CORNER)):
            send(kind, s, dep_out.at[s, pl.ds(part * cells_y, cells_y)], dep_in.at[s, part])
        turned = picked(turn[s + 1], fresh[...], 3)
        if s + 1 < STEPS:
            send_rv(s + 1, turned)
        else:
            out_radius[...] = turned[:, :BIN]
            out_velocity[...] = turned[:, BIN:]
        if s + 1 < STEPS:
            fix[s + 1] = merged(FIX_UP, FIX_DOWN, s + 1, fix_in, fix_out)
            if s + 2 < STEPS:
                send_fix(s + 2, picked(turn[s + 2], fix[s + 1], 3))

        for kind in (X_LOW, Y_LOW):
            arrive(kind, s, halo.at[s, kind])
        after = out_pressure if s + 1 == STEPS else field.at[s]
        y_at, z_at = iota((cells_y, depth), 0), iota((cells_y, depth), 1)
        bases = []
        for x in range(cells_x):
            here = now[x]
            around = (halo[s, X_LOW] if x == 0 else now[x - 1]) + (
                halo[s, X_HIGH] if x == cells_x - 1 else now[x + 1]
            )
            around = around + jnp.where(
                y_at == 0, halo[s, Y_LOW, x : x + 1, :], pltpu.roll(here, 1, 0)
            )
            around = around + jnp.where(
                y_at == cells_y - 1, halo[s, Y_HIGH, x : x + 1, :], pltpu.roll(here, cells_y - 1, 0)
            )
            around = around + jnp.where(z_at == 0, 0.0, pltpu.roll(here, 1, 1))
            around = around + jnp.where(z_at == depth - 1, 0.0, pltpu.roll(here, depth - 1, 1))
            bases.append(
                2.0 * here
                - before[x]
                + courant_square * (around - 6.0 * here)
                + source_gain * collected[x * cells_y : (x + 1) * cells_y, :]
            )
        for part, kind in enumerate((DEP_X, DEP_Y, DEP_CORNER)):
            arrive(kind, s, dep_in.at[s, part])
        for x in range(cells_x):
            extra = jnp.where(y_at == 0, dep_in[s, 1, x : x + 1, :], 0.0)
            if x == 0:
                extra = extra + dep_in[s, 0] + dep_in[s, 2]
            after[x] = bases[x] + source_gain * extra
        if s + 1 < STEPS:
            send_halo(s + 1, after)

    for there, made in pending:

        @pl.when(there)
        def _():
            made.wait_send()


def local(
    slabs, bricks,
    pressure, previous, radius, velocity, positions, occupancy, anchors, migrations, crossings,
):
    cells_x, cells_y, depth = pressure.shape
    bins = radius.shape[0]
    most = bins // 2
    vmem = pl.BlockSpec(memory_space=pltpu.VMEM)
    smem = pl.BlockSpec(memory_space=pltpu.SMEM)
    scratch = [
        pltpu.VMEM((STEPS, 5, cells_y, depth), F32),
        pltpu.VMEM((STEPS, 2, cells_y, depth), F32),
        pltpu.VMEM((STEPS, 3, cells_y, depth), F32),
        pltpu.VMEM((STEPS, 3 * cells_y, depth), F32),
        pltpu.VMEM((STEPS, 2, most, 4 * BIN), F32),
        pltpu.VMEM((STEPS, bins, 4 * BIN), F32),
        pltpu.VMEM((STEPS, bins, 4 * BIN), F32),
        pltpu.VMEM((STEPS, 2, most, 2 * BIN), F32),
        pltpu.VMEM((STEPS, bins, 2 * BIN), F32),
        pltpu.VMEM((bins, 2 * BIN), F32),
        pltpu.VMEM((2, 8, 128), jnp.int32),
        pltpu.VMEM((STEPS - 1, cells_x, cells_y, depth), F32),
        pltpu.VMEM((4 * bins, depth), F32),
        pltpu.VMEM((4 * bins, depth), F32),
        pltpu.VMEM((bins, 2 * BIN), F32),
        pltpu.VMEM((STEPS, bins, BIN), jnp.int32),
        pltpu.VMEM((STEPS, 4 * bins, 128), BF16),
        pltpu.VMEM((STEPS, 128, 4 * bins), BF16),
        pltpu.VMEM((STEPS + 1, bins, bins), BF16),
        pltpu.SemaphoreType.DMA((STEPS, KINDS)),
        pltpu.SemaphoreType.DMA((STEPS, KINDS)),
    ]
    return pl.pallas_call(
        functools.partial(kernel, slabs, bricks),
        out_shape=(
            jax.ShapeDtypeStruct(pressure.shape, F32),
            jax.ShapeDtypeStruct(radius.shape, F32),
            jax.ShapeDtypeStruct(velocity.shape, F32),
        ),
        in_specs=[vmem] * 8 + [smem],
        out_specs=(vmem,) * 3,
        scratch_shapes=scratch,
        compiler_params=pltpu.CompilerParams(
            collective_id=0, has_side_effects=True, vmem_limit_bytes=24 * 1024 * 1024
        ),
    )(
        pressure, previous, radius, velocity, positions, occupancy.reshape(1, bins), anchors,
        migrations, crossings,
    )


def solution(mesh):
    placed = (
        P("slab", "brick", None),
        P("slab", "brick", None),
        P(("slab", "brick"), None),
        P(("slab", "brick"), None),
        P(None, ("slab", "brick"), None),
        P(("slab", "brick")),
        P(None, None, ("slab", "brick")),
        P(None, ("slab", "brick")),
        P(None, ("slab", "brick")),
    )
    return jax.shard_map(
        functools.partial(local, mesh.shape["slab"], mesh.shape["brick"]),
        mesh=mesh,
        in_specs=placed,
        out_specs=(
            P("slab", "brick", None),
            P(("slab", "brick"), None),
            P(("slab", "brick"), None),
        ),
        check_vma=False,
    )
```

```python
import functools

import jax
import jax.numpy as jnp
from jax import lax
from jax.experimental import pallas as pl
from jax.experimental.pallas import tpu as pltpu
from jax.sharding import PartitionSpec as P

BIN = 128
PZ = 32
STEPS = 3

courant_square = 0.25
source_gain = 0.05
kernel_width = 2.25
gas_pressure = 1.2
surface_tension = 0.1
viscosity = 0.02
polytropic = 1.4
sound_speed = 20.0
drive_gain = 0.5
time_step = 0.05
four_pi = 12.566370614359172
root = (1.4426950408889634 / (2.0 * kernel_width)) ** 0.5

MESH = pl.DeviceIdType.MESH
F32 = jnp.float32
BF16 = jnp.bfloat16

X_HIGH, X_LOW, Y_HIGH, Y_LOW, CORNER = range(5)
DEP_X, DEP_Y, DEP_CORNER = range(5, 8)
FIX_UP, FIX_DOWN, RV_UP, RV_DOWN, COUNT = range(8, 13)
OFFSETS = (
    (-1, 0), (1, 0), (0, -1), (0, 1), (-1, -1),
    (1, 0), (0, 1), (1, 1),
    (0, 1), (0, -1), (0, 1), (0, -1), (0, 1),
)
KINDS = len(OFFSETS)


def pieces(value, count):
    found = []
    for _ in range(count - 1):
        piece = value.astype(BF16)
        found.append(piece)
        value = value - piece.astype(F32)
    found.append(value.astype(BF16))
    return found


def picked(one_hot, value, count):
    total = None
    for piece in pieces(value, count):
        term = jnp.dot(one_hot, piece, preferred_element_type=F32)
        total = term if total is None else total + term
    return total


def wall_accel(radius, velocity, outside):
    gas_term = gas_pressure * jnp.exp(-3.0 * polytropic * jnp.log(radius))
    inverse = 1.0 / radius
    wall_term = gas_term - (2.0 * surface_tension + 4.0 * viscosity * velocity) * inverse
    ambient = 1.0 + drive_gain * outside
    mach_number = velocity * (1.0 / sound_speed)
    driving = (1.0 + mach_number) * (wall_term - ambient) - 1.5 * (
        1.0 - mach_number * (1.0 / 3.0)
    ) * velocity * velocity
    return driving / ((1.0 - mach_number) * radius)


def iota(shape, dim):
    return lax.broadcasted_iota(jnp.int32, shape, dim)


def pair_factor(fraction):
    low = jnp.exp2(-jnp.square(fraction * root))
    high = jnp.exp2(-jnp.square((fraction - 1.0) * root))
    total = 1.0 / (low + high)
    return low * total, high * total


def kernel(
    slabs, bricks,
    pressure_hbm, previous_hbm, radius_hbm, velocity_hbm, positions_hbm, occupancy_hbm,
    anchors_hbm, migrations_hbm, crossings_hbm,
    out_pressure, out_radius, out_velocity,
    pressure, previous, radius, velocity, positions, occupancy, anchors, migrations, crossings,
    halo, edge, dep_in, dep_out, fix_in, fix_out, fix, rv_in, rv_out, rv, counts, field,
    rows, placed, fresh, corner_z, take, put, turn, parts, shares, planar, norms, w_high, w_low,
    send_sem, recv_sem, load_sem,
):
    loads = {}
    for index, (name, source, target) in enumerate(
        (
            ("migrations", migrations_hbm, migrations),
            ("radius", radius_hbm, radius),
            ("velocity", velocity_hbm, velocity),
            ("positions", positions_hbm, positions),
            ("occupancy", occupancy_hbm, occupancy),
            ("pressure", pressure_hbm, pressure),
            ("crossings", crossings_hbm, crossings),
            ("anchors", anchors_hbm, anchors),
            ("previous", previous_hbm, previous),
        )
    ):
        loads[name] = pltpu.make_async_copy(source, target, load_sem.at[index])
        loads[name].start()

    cells_x, cells_y, depth = pressure.shape
    bins = radius.shape[0]
    most = bins // 2
    own = cells_x * cells_y
    slab, brick = lax.axis_index("slab"), lax.axis_index("brick")

    def inside(dx, dy):
        a, b = slab + dx, brick + dy
        return (a >= 0) & (a < slabs) & (b >= 0) & (b < bricks)

    barrier = pltpu.get_barrier_semaphore()
    near = ((1, 0), (-1, 0), (0, 1), (0, -1), (1, 1), (-1, -1))
    expected = jnp.int32(0)
    for dx, dy in near:
        expected = expected + inside(dx, dy).astype(jnp.int32)

        @pl.when(inside(dx, dy))
        def _():
            pl.semaphore_signal(
                barrier, inc=1, device_id=(slab + dx, brick + dy), device_id_type=MESH
            )

    pending = []

    def copy(kind, step, source, target):
        dx, dy = OFFSETS[kind]
        return pltpu.make_async_remote_copy(
            src_ref=source,
            dst_ref=target,
            send_sem=send_sem.at[step, kind],
            recv_sem=recv_sem.at[step, kind],
            device_id=(slab + dx, brick + dy),
            device_id_type=MESH,
        )

    def send(kind, step, source, target):
        made = copy(kind, step, source, target)
        there = inside(*OFFSETS[kind])

        @pl.when(there)
        def _():
            made.start()

        pending.append((there, made))

    def arrive(kind, step, target):
        dx, dy = OFFSETS[kind]

        @pl.when(inside(-dx, -dy))
        def _():
            copy(kind, step, target, target).wait_recv()

    loads["migrations"].wait()
    eye = iota((bins, bins), 0) == iota((bins, bins), 1)

    def column(row):
        return jnp.sum(jnp.where(eye, jnp.broadcast_to(row, (bins, bins)), 0.0), axis=1, keepdims=True)

    slot_row = iota((1, bins), 1).astype(F32)
    slot_column = iota((bins, 1), 0).astype(F32)
    list_rows = [migrations[s : s + 1, :].astype(F32) for s in range(STEPS)]
    list_columns = [column(row) for row in list_rows]

    def turn_of(s):
        before = slot_row if s == 0 else list_rows[s - 1]
        after = slot_column if s == STEPS else list_columns[s]
        return (after == before).astype(F32).astype(BF16)

    def send_fix(s, value):
        fix_out[s] = value
        send(FIX_UP, s, fix_out.at[s, pl.ds(most, most)], fix_in.at[s, 0])
        send(FIX_DOWN, s, fix_out.at[s, pl.ds(0, most)], fix_in.at[s, 1])

    def send_rv(s, value):
        rv_out[s] = value
        send(RV_UP, s, rv_out.at[s, pl.ds(most, most)], rv_in.at[s, 0])
        send(RV_DOWN, s, rv_out.at[s, pl.ds(0, most)], rv_in.at[s, 1])

    def send_halo(s, block):
        edge[s, 0] = jnp.concatenate([block[x, 0:1, :] for x in range(cells_x)], axis=0)
        edge[s, 1] = jnp.concatenate(
            [block[x, cells_y - 1 : cells_y, :] for x in range(cells_x)], axis=0
        )
        send(X_HIGH, s, block.at[0], halo.at[s, X_HIGH])
        send(X_LOW, s, block.at[cells_x - 1], halo.at[s, X_LOW])
        send(Y_HIGH, s, edge.at[s, 0], halo.at[s, Y_HIGH])
        send(Y_LOW, s, edge.at[s, 1], halo.at[s, Y_LOW])
        send(CORNER, s, block.at[0], halo.at[s, CORNER])

    listed = iota((most, 1), 0)

    def merged(kind_up, kind_down, s, arrived, sent):
        arrive(kind_up, s, arrived.at[s, 0])
        arrive(kind_down, s, arrived.at[s, 1])
        width = sent.shape[2]
        from_below = jnp.broadcast_to(listed < counts[1, s : s + 1, 0:1], (most, width))
        from_above = jnp.broadcast_to(listed < counts[0, s : s + 1, 0:1], (most, width))
        return jnp.concatenate(
            [
                jnp.where(from_below, arrived[s, 0], sent[s, 0:most, :]),
                jnp.where(from_above, arrived[s, 1], sent[s, most:bins, :]),
            ],
            axis=0,
        )

    count_row = iota((8, 128), 0)

    for kind in range(5):
        dx, dy = OFFSETS[kind]

        @pl.when(jnp.logical_not(inside(-dx, -dy)))
        def _():
            for s in range(STEPS):
                halo[s, kind] = jnp.zeros((cells_y, depth), F32)

    for kind in (DEP_X, DEP_Y, DEP_CORNER):
        dx, dy = OFFSETS[kind]

        @pl.when(jnp.logical_not(inside(-dx, -dy)))
        def _():
            for s in range(STEPS):
                dep_in[s, kind - 5] = jnp.zeros((cells_y, depth), F32)

    @pl.when(brick == 0)
    def _():
        counts[1] = jnp.zeros((8, 128), jnp.int32)

    for name in ("radius", "velocity", "positions", "occupancy", "pressure", "crossings"):
        loads[name].wait()
    my_counts = jnp.zeros((8, 128), jnp.int32)
    for s in range(STEPS):
        my_counts = jnp.where(
            count_row == s, jnp.broadcast_to(crossings[s : s + 1, :], (8, 128)), my_counts
        )
    counts[0] = my_counts
    alive = jnp.broadcast_to(column(occupancy[...].astype(F32)), (bins, BIN))
    first = jnp.concatenate(
        [radius[...], velocity[...], positions[0], positions[1], positions[2], alive], axis=1
    )
    first = picked(turn_of(0), first, 3)

    pl.semaphore_wait(barrier, expected)
    counts_copy = copy(COUNT, 0, counts.at[0], counts.at[1])
    there = inside(*OFFSETS[COUNT])

    @pl.when(there)
    def _():
        counts_copy.start()

    pending.append((there, counts_copy))
    send_fix(0, first[:, 2 * BIN :])
    send_halo(0, pressure)
    send_rv(0, first[:, : 2 * BIN])

    loads["anchors"].wait()
    patch_rows = 4 * bins
    owner = iota((patch_rows, bins), 0) // 4 == iota((patch_rows, bins), 1)
    which = iota((patch_rows, 1), 0) % 4
    square = iota((patch_rows, patch_rows), 0) == iota((patch_rows, patch_rows), 1)
    for s in range(STEPS):
        turn[s + 1] = turn_of(s + 1)
        listed_slot = jnp.sum(jnp.where(owner, list_rows[s], 0.0), axis=1, keepdims=True)
        chosen = listed_slot == slot_row
        x, y, z = [
            jnp.sum(
                jnp.where(chosen, anchors[s, d : d + 1, :].astype(F32), 0.0), axis=1, keepdims=True
            ).astype(jnp.int32)
            for d in range(3)
        ]
        corner_z[s] = jnp.broadcast_to(z, (patch_rows, BIN))
        x, y = x + which // 2, y + which % 2
        cells = jnp.where(y < cells_y, x * cells_y + y, own + cells_y + x)
        take[s] = (iota((patch_rows, 128), 1) == cells).astype(F32).astype(BF16)
        cells = jnp.sum(jnp.where(square, cells.astype(F32), 0.0), axis=0, keepdims=True)
        put[s] = (iota((128, patch_rows), 0).astype(F32) == cells).astype(F32).astype(BF16)

    far = iota((PZ, BIN), 0).astype(F32) * root

    def build_weights(s):
        def group(index, carry):
            at = pl.ds(pl.multiple_of(index * 8, 8), 8)
            scaled = fix[s, at, 2 * BIN : 3 * BIN] * ((PZ - 1.0) * root)
            totals = []
            for g in range(8):
                weight = jnp.exp2(-jnp.square(scaled[g : g + 1, :] - far))
                totals.append(jnp.sum(weight, axis=0, keepdims=True))
                those = pl.ds(pl.multiple_of(index * (8 * PZ) + g * PZ, PZ), PZ)
                high = weight.astype(BF16)
                w_high[those, :] = high
                w_low[those, :] = (weight - high.astype(F32)).astype(BF16)
            norms[at, :] = jnp.concatenate(totals, axis=0)
            return carry

        lax.fori_loop(0, bins // 8, group, 0)
        x_pair = pair_factor(fix[s, :, 0:BIN])
        y_pair = pair_factor(fix[s, :, BIN : 2 * BIN])
        norm = 1.0 / norms[...]
        for c in range(4):
            planar[c] = x_pair[c // 2] * (y_pair[c % 2] * norm)

    arrive(COUNT, 0, counts.at[1])
    fix[0] = merged(FIX_UP, FIX_DOWN, 0, fix_in, fix_out)
    send_fix(1, picked(turn[1], fix[0], 3))
    build_weights(0)
    loads["previous"].wait()

    lane = iota((8, 128), 1)
    bin_in_four = [2 * h + iota((8, 128), 0) // 4 for h in range(2)]
    nt = (((1,), (1,)), ((), ()))
    for s in range(STEPS):
        now = pressure if s == 0 else field.at[s - 1]
        before = previous if s == 0 else (pressure if s == 1 else field.at[s - 2])
        for kind in (X_HIGH, Y_HIGH, CORNER):
            arrive(kind, s, halo.at[s, kind])
        corner_row = jnp.where(iota((cells_y, depth), 0) == 0, halo[s, CORNER], 0.0)
        cells = jnp.concatenate(
            [
                now[...].reshape(own, depth),
                halo[s, X_HIGH],
                halo[s, Y_HIGH],
                corner_row,
                jnp.zeros((128 - own - 3 * cells_y, depth), F32),
            ],
            axis=0,
        )
        rows[...] = picked(take[s], cells, 2)
        rv[...] = merged(RV_UP, RV_DOWN, s, rv_in, rv_out)

        for q in range(bins // 4):
            halves = []
            for h in range(2):
                at = slice(16 * q + 8 * h, 16 * q + 8 * h + 8)
                z = corner_z[s, at, :] + lane % PZ
                found = [
                    jnp.take_along_axis(
                        rows[at, 128 * part : 128 * (part + 1)],
                        z % 128,
                        axis=1,
                        mode="promise_in_bounds",
                    )
                    for part in range(depth // 128)
                ]
                patch = jnp.where(z >= 128, found[1], found[0])
                halves.append(jnp.where(lane // PZ == bin_in_four[h], patch, 0.0))
            high, low = pieces(jnp.concatenate(halves, axis=0), 2)
            four = slice(128 * q, 128 * (q + 1))
            parts[16 * q : 16 * (q + 1), :] = (
                jnp.dot(high, w_high[four, :], preferred_element_type=F32)
                + jnp.dot(low, w_high[four, :], preferred_element_type=F32)
                + jnp.dot(high, w_low[four, :], preferred_element_type=F32)
            )
        outside = None
        for c in range(4):
            term = planar[c] * parts[pl.ds(c, bins, stride=4), :]
            outside = term if outside is None else outside + term
        r, v = rv[:, 0:BIN], rv[:, BIN : 2 * BIN]
        first_accel = wall_accel(r, v, outside)
        mid_r = r + 0.5 * time_step * v
        mid_v = v + 0.5 * time_step * first_accel
        second_accel = wall_accel(mid_r, mid_v, outside)
        fresh[:, 0:BIN] = r + time_step * mid_v
        fresh[:, BIN : 2 * BIN] = v + time_step * second_accel
        volume = four_pi * (2.0 * mid_r * mid_v * mid_v + mid_r * mid_r * second_accel)
        live = iota((bins, BIN), 1).astype(F32) < fix[s, :, 3 * BIN : 4 * BIN]
        volume = jnp.where(live, volume, 0.0)
        for c in range(4):
            shares[pl.ds(c, bins, stride=4), :] = planar[c] * volume
        for q in range(bins // 4):
            high, low = pieces(shares[16 * q : 16 * (q + 1), :], 2)
            four = slice(128 * q, 128 * (q + 1))
            given = (
                lax.dot_general(high, w_high[four, :], nt, preferred_element_type=F32)
                + lax.dot_general(low, w_high[four, :], nt, preferred_element_type=F32)
                + lax.dot_general(high, w_low[four, :], nt, preferred_element_type=F32)
            )
            for h in range(2):
                at = slice(16 * q + 8 * h, 16 * q + 8 * h + 8)
                for part in range(depth // 128):
                    away = lane + 128 * part - corner_z[s, at, :]
                    valid = (away >= 0) & (away < PZ)
                    found = jnp.take_along_axis(
                        given[8 * h : 8 * h + 8, :],
                        jnp.clip(away, 0, PZ - 1) + PZ * bin_in_four[h],
                        axis=1,
                        mode="promise_in_bounds",
                    )
                    placed[at, 128 * part : 128 * (part + 1)] = jnp.where(valid, found, 0.0)

        collected = picked(put[s], placed[...], 2)
        dep_out[s] = collected[own : own + 3 * cells_y, :]
        for part, kind in enumerate((DEP_X, DEP_Y, DEP_CORNER)):
            send(kind, s, dep_out.at[s, pl.ds(part * cells_y, cells_y)], dep_in.at[s, part])
        turned = picked(turn[s + 1], fresh[...], 3)
        if s + 1 < STEPS:
            send_rv(s + 1, turned)
        else:
            out_radius[...] = turned[:, :BIN]
            out_velocity[...] = turned[:, BIN:]
        if s + 1 < STEPS:
            fix[s + 1] = merged(FIX_UP, FIX_DOWN, s + 1, fix_in, fix_out)
            if s + 2 < STEPS:
                send_fix(s + 2, picked(turn[s + 2], fix[s + 1], 3))
            build_weights(s + 1)

        for kind in (X_LOW, Y_LOW):
            arrive(kind, s, halo.at[s, kind])
        after = out_pressure if s + 1 == STEPS else field.at[s]
        y_at, z_at = iota((cells_y, depth), 0), iota((cells_y, depth), 1)
        bases = []
        for x in range(cells_x):
            here = now[x]
            around = (halo[s, X_LOW] if x == 0 else now[x - 1]) + (
                halo[s, X_HIGH] if x == cells_x - 1 else now[x + 1]
            )
            around = around + jnp.where(
                y_at == 0, halo[s, Y_LOW, x : x + 1, :], pltpu.roll(here, 1, 0)
            )
            around = around + jnp.where(
                y_at == cells_y - 1, halo[s, Y_HIGH, x : x + 1, :], pltpu.roll(here, cells_y - 1, 0)
            )
            around = around + jnp.where(z_at == 0, 0.0, pltpu.roll(here, 1, 1))
            around = around + jnp.where(z_at == depth - 1, 0.0, pltpu.roll(here, depth - 1, 1))
            bases.append(
                2.0 * here
                - before[x]
                + courant_square * (around - 6.0 * here)
                + source_gain * collected[x * cells_y : (x + 1) * cells_y, :]
            )
        for part, kind in enumerate((DEP_X, DEP_Y, DEP_CORNER)):
            arrive(kind, s, dep_in.at[s, part])
        for x in range(cells_x):
            extra = jnp.where(y_at == 0, dep_in[s, 1, x : x + 1, :], 0.0)
            if x == 0:
                extra = extra + dep_in[s, 0] + dep_in[s, 2]
            after[x] = bases[x] + source_gain * extra
        if s + 1 < STEPS:
            send_halo(s + 1, after)

    for there, made in pending:

        @pl.when(there)
        def _():
            made.wait_send()


def local(
    slabs, bricks,
    pressure, previous, radius, velocity, positions, occupancy, anchors, migrations, crossings,
):
    cells_x, cells_y, depth = pressure.shape
    bins = radius.shape[0]
    most = bins // 2
    vmem = pl.BlockSpec(memory_space=pltpu.VMEM)
    hbm = pl.BlockSpec(memory_space=pltpu.HBM)
    scratch = [
        pltpu.VMEM(pressure.shape, F32),
        pltpu.VMEM(previous.shape, F32),
        pltpu.VMEM(radius.shape, F32),
        pltpu.VMEM(velocity.shape, F32),
        pltpu.VMEM(positions.shape, F32),
        pltpu.VMEM((1, bins), jnp.int32),
        pltpu.VMEM(anchors.shape, jnp.int32),
        pltpu.VMEM(migrations.shape, jnp.int32),
        pltpu.VMEM(crossings.shape, jnp.int32),
        pltpu.VMEM((STEPS, 5, cells_y, depth), F32),
        pltpu.VMEM((STEPS, 2, cells_y, depth), F32),
        pltpu.VMEM((STEPS, 3, cells_y, depth), F32),
        pltpu.VMEM((STEPS, 3 * cells_y, depth), F32),
        pltpu.VMEM((STEPS, 2, most, 4 * BIN), F32),
        pltpu.VMEM((STEPS, bins, 4 * BIN), F32),
        pltpu.VMEM((STEPS, bins, 4 * BIN), F32),
        pltpu.VMEM((STEPS, 2, most, 2 * BIN), F32),
        pltpu.VMEM((STEPS, bins, 2 * BIN), F32),
        pltpu.VMEM((bins, 2 * BIN), F32),
        pltpu.VMEM((2, 8, 128), jnp.int32),
        pltpu.VMEM((STEPS - 1, cells_x, cells_y, depth), F32),
        pltpu.VMEM((4 * bins, depth), F32),
        pltpu.VMEM((4 * bins, depth), F32),
        pltpu.VMEM((bins, 2 * BIN), F32),
        pltpu.VMEM((STEPS, 4 * bins, BIN), jnp.int32),
        pltpu.VMEM((STEPS, 4 * bins, 128), BF16),
        pltpu.VMEM((STEPS, 128, 4 * bins), BF16),
        pltpu.VMEM((STEPS + 1, bins, bins), BF16),
        pltpu.VMEM((4 * bins, BIN), F32),
        pltpu.VMEM((4 * bins, BIN), F32),
        pltpu.VMEM((4, bins, BIN), F32),
        pltpu.VMEM((bins, BIN), F32),
        pltpu.VMEM((PZ * bins, BIN), BF16),
        pltpu.VMEM((PZ * bins, BIN), BF16),
        pltpu.SemaphoreType.DMA((STEPS, KINDS)),
        pltpu.SemaphoreType.DMA((STEPS, KINDS)),
        pltpu.SemaphoreType.DMA((9,)),
    ]
    return pl.pallas_call(
        functools.partial(kernel, slabs, bricks),
        out_shape=(
            jax.ShapeDtypeStruct(pressure.shape, F32),
            jax.ShapeDtypeStruct(radius.shape, F32),
            jax.ShapeDtypeStruct(velocity.shape, F32),
        ),
        in_specs=[hbm] * 9,
        out_specs=(vmem,) * 3,
        scratch_shapes=scratch,
        compiler_params=pltpu.CompilerParams(
            collective_id=0, has_side_effects=True, vmem_limit_bytes=24 * 1024 * 1024
        ),
    )(
        pressure, previous, radius, velocity, positions, occupancy.reshape(1, bins), anchors,
        migrations, crossings,
    )


def solution(mesh):
    placed = (
        P("slab", "brick", None),
        P("slab", "brick", None),
        P(("slab", "brick"), None),
        P(("slab", "brick"), None),
        P(None, ("slab", "brick"), None),
        P(("slab", "brick")),
        P(None, None, ("slab", "brick")),
        P(None, ("slab", "brick")),
        P(None, ("slab", "brick")),
    )
    return jax.shard_map(
        functools.partial(local, mesh.shape["slab"], mesh.shape["brick"]),
        mesh=mesh,
        in_specs=placed,
        out_specs=(
            P("slab", "brick", None),
            P(("slab", "brick"), None),
            P(("slab", "brick"), None),
        ),
        check_vma=False,
    )
```

```python
import functools

import jax
import jax.numpy as jnp
from jax import lax
from jax.experimental import pallas as pl
from jax.experimental.pallas import tpu as pltpu
from jax.sharding import PartitionSpec as P

BIN = 128
PZ = 32
STEPS = 3

courant_square = 0.25
source_gain = 0.05
kernel_width = 2.25
gas_pressure = 1.2
surface_tension = 0.1
viscosity = 0.02
polytropic = 1.4
sound_speed = 20.0
drive_gain = 0.5
time_step = 0.05
four_pi = 12.566370614359172
root = (1.4426950408889634 / (2.0 * kernel_width)) ** 0.5

MESH = pl.DeviceIdType.MESH
F32 = jnp.float32
BF16 = jnp.bfloat16

X_HIGH, X_LOW, Y_HIGH, Y_LOW, CORNER = range(5)
DEP_X, DEP_Y, DEP_CORNER = range(5, 8)
FIX_UP, FIX_DOWN, RV_UP, RV_DOWN, COUNT = range(8, 13)
OFFSETS = (
    (-1, 0), (1, 0), (0, -1), (0, 1), (-1, -1),
    (1, 0), (0, 1), (1, 1),
    (0, 1), (0, -1), (0, 1), (0, -1), (0, 1),
)
KINDS = len(OFFSETS)


def pieces(value, count):
    found = []
    for _ in range(count - 1):
        piece = value.astype(BF16)
        found.append(piece)
        value = value - piece.astype(F32)
    found.append(value.astype(BF16))
    return found


def picked(one_hot, value, count):
    total = None
    for piece in pieces(value, count):
        term = jnp.dot(one_hot, piece, preferred_element_type=F32)
        total = term if total is None else total + term
    return total


def wall_accel(radius, velocity, outside):
    gas_term = gas_pressure * jnp.exp(-3.0 * polytropic * jnp.log(radius))
    inverse = 1.0 / radius
    wall_term = gas_term - (2.0 * surface_tension + 4.0 * viscosity * velocity) * inverse
    ambient = 1.0 + drive_gain * outside
    mach_number = velocity * (1.0 / sound_speed)
    driving = (1.0 + mach_number) * (wall_term - ambient) - 1.5 * (
        1.0 - mach_number * (1.0 / 3.0)
    ) * velocity * velocity
    return driving / ((1.0 - mach_number) * radius)


def iota(shape, dim):
    return lax.broadcasted_iota(jnp.int32, shape, dim)


def pair_factor(fraction):
    low = jnp.exp2(-jnp.square(fraction * root))
    high = jnp.exp2(-jnp.square((fraction - 1.0) * root))
    total = 1.0 / (low + high)
    return low * total, high * total


def kernel(
    slabs, bricks,
    pressure_hbm, previous_hbm, radius_hbm, velocity_hbm, positions_hbm, occupancy_hbm,
    anchors_hbm, migrations_hbm, crossings_hbm,
    out_pressure, out_radius, out_velocity,
    pressure, previous, radius, velocity, positions, occupancy, anchors, migrations, crossings,
    halo, edge, dep_in, dep_out, fix_in, fix_out, fix, rv_in, rv_out, rv, counts, field,
    rows, placed, fresh, corner_z, take, put, turn, parts, shares, planar, norms, w_high, w_low,
    send_sem, recv_sem, load_sem,
):
    loads = {}
    for index, (name, source, target) in enumerate(
        (
            ("migrations", migrations_hbm, migrations),
            ("radius", radius_hbm, radius),
            ("velocity", velocity_hbm, velocity),
            ("positions", positions_hbm, positions),
            ("occupancy", occupancy_hbm, occupancy),
            ("pressure", pressure_hbm, pressure),
            ("crossings", crossings_hbm, crossings),
            ("anchors", anchors_hbm, anchors),
            ("previous", previous_hbm, previous),
        )
    ):
        loads[name] = pltpu.make_async_copy(source, target, load_sem.at[index])
        loads[name].start()

    cells_x, cells_y, depth = pressure.shape
    bins = radius.shape[0]
    most = bins // 2
    own = cells_x * cells_y
    slab, brick = lax.axis_index("slab"), lax.axis_index("brick")

    def inside(dx, dy):
        a, b = slab + dx, brick + dy
        return (a >= 0) & (a < slabs) & (b >= 0) & (b < bricks)

    barrier = pltpu.get_barrier_semaphore()
    near = ((1, 0), (-1, 0), (0, 1), (0, -1), (1, 1), (-1, -1))
    expected = jnp.int32(0)
    for dx, dy in near:
        expected = expected + inside(dx, dy).astype(jnp.int32)

        @pl.when(inside(dx, dy))
        def _():
            pl.semaphore_signal(
                barrier, inc=1, device_id=(slab + dx, brick + dy), device_id_type=MESH
            )

    pending = []

    def copy(kind, step, source, target):
        dx, dy = OFFSETS[kind]
        return pltpu.make_async_remote_copy(
            src_ref=source,
            dst_ref=target,
            send_sem=send_sem.at[step, kind],
            recv_sem=recv_sem.at[step, kind],
            device_id=(slab + dx, brick + dy),
            device_id_type=MESH,
        )

    def send(kind, step, source, target):
        made = copy(kind, step, source, target)
        there = inside(*OFFSETS[kind])

        @pl.when(there)
        def _():
            made.start()

        pending.append((there, made))

    def arrive(kind, step, target):
        dx, dy = OFFSETS[kind]

        @pl.when(inside(-dx, -dy))
        def _():
            copy(kind, step, target, target).wait_recv()

    loads["migrations"].wait()
    eye = iota((bins, bins), 0) == iota((bins, bins), 1)

    def column(row):
        return jnp.sum(jnp.where(eye, jnp.broadcast_to(row, (bins, bins)), 0.0), axis=1, keepdims=True)

    slot_row = iota((1, bins), 1).astype(F32)
    slot_column = iota((bins, 1), 0).astype(F32)
    list_rows = [migrations[s : s + 1, :].astype(F32) for s in range(STEPS)]
    list_columns = [column(row) for row in list_rows]

    def turn_of(s):
        before = slot_row if s == 0 else list_rows[s - 1]
        after = slot_column if s == STEPS else list_columns[s]
        return (after == before).astype(F32).astype(BF16)

    def send_fix(s, value):
        fix_out[s] = value
        send(FIX_UP, s, fix_out.at[s, pl.ds(most, most)], fix_in.at[s, 0])
        send(FIX_DOWN, s, fix_out.at[s, pl.ds(0, most)], fix_in.at[s, 1])

    def send_rv(s, value):
        rv_out[s] = value
        send(RV_UP, s, rv_out.at[s, pl.ds(most, most)], rv_in.at[s, 0])
        send(RV_DOWN, s, rv_out.at[s, pl.ds(0, most)], rv_in.at[s, 1])

    def send_halo(s, block):
        edge[s, 0] = jnp.concatenate([block[x, 0:1, :] for x in range(cells_x)], axis=0)
        edge[s, 1] = jnp.concatenate(
            [block[x, cells_y - 1 : cells_y, :] for x in range(cells_x)], axis=0
        )
        send(X_HIGH, s, block.at[0], halo.at[s, X_HIGH])
        send(X_LOW, s, block.at[cells_x - 1], halo.at[s, X_LOW])
        send(Y_HIGH, s, edge.at[s, 0], halo.at[s, Y_HIGH])
        send(Y_LOW, s, edge.at[s, 1], halo.at[s, Y_LOW])
        send(CORNER, s, block.at[0], halo.at[s, CORNER])

    listed = iota((most, 1), 0)

    def merged(kind_up, kind_down, s, arrived, sent):
        arrive(kind_up, s, arrived.at[s, 0])
        arrive(kind_down, s, arrived.at[s, 1])
        width = sent.shape[2]
        from_below = jnp.broadcast_to(listed < counts[1, s : s + 1, 0:1], (most, width))
        from_above = jnp.broadcast_to(listed < counts[0, s : s + 1, 0:1], (most, width))
        return jnp.concatenate(
            [
                jnp.where(from_below, arrived[s, 0], sent[s, 0:most, :]),
                jnp.where(from_above, arrived[s, 1], sent[s, most:bins, :]),
            ],
            axis=0,
        )

    count_row = iota((8, 128), 0)

    for kind in range(5):
        dx, dy = OFFSETS[kind]

        @pl.when(jnp.logical_not(inside(-dx, -dy)))
        def _():
            for s in range(STEPS):
                halo[s, kind] = jnp.zeros((cells_y, depth), F32)

    for kind in (DEP_X, DEP_Y, DEP_CORNER):
        dx, dy = OFFSETS[kind]

        @pl.when(jnp.logical_not(inside(-dx, -dy)))
        def _():
            for s in range(STEPS):
                dep_in[s, kind - 5] = jnp.zeros((cells_y, depth), F32)

    @pl.when(brick == 0)
    def _():
        counts[1] = jnp.zeros((8, 128), jnp.int32)

    for name in ("radius", "velocity", "positions", "occupancy", "pressure", "crossings"):
        loads[name].wait()
    my_counts = jnp.zeros((8, 128), jnp.int32)
    for s in range(STEPS):
        my_counts = jnp.where(
            count_row == s, jnp.broadcast_to(crossings[:, s : s + 1], (8, 128)), my_counts
        )
    counts[0] = my_counts
    alive = jnp.broadcast_to(column(occupancy[...].astype(F32)), (bins, BIN))
    first = jnp.concatenate(
        [radius[...], velocity[...], positions[0], positions[1], positions[2], alive], axis=1
    )
    first = picked(turn_of(0), first, 3)

    pl.semaphore_wait(barrier, expected)
    counts_copy = copy(COUNT, 0, counts.at[0], counts.at[1])
    there = inside(*OFFSETS[COUNT])

    @pl.when(there)
    def _():
        counts_copy.start()

    pending.append((there, counts_copy))
    send_fix(0, first[:, 2 * BIN :])
    send_halo(0, pressure)
    send_rv(0, first[:, : 2 * BIN])

    loads["anchors"].wait()
    patch_rows = 4 * bins
    owner = iota((patch_rows, bins), 0) // 4 == iota((patch_rows, bins), 1)
    which = iota((patch_rows, 1), 0) % 4
    square = iota((patch_rows, patch_rows), 0) == iota((patch_rows, patch_rows), 1)
    for s in range(STEPS):
        turn[s + 1] = turn_of(s + 1)
        listed_slot = jnp.sum(jnp.where(owner, list_rows[s], 0.0), axis=1, keepdims=True)
        chosen = listed_slot == slot_row
        x, y, z = [
            jnp.sum(
                jnp.where(chosen, anchors[s, d : d + 1, :].astype(F32), 0.0), axis=1, keepdims=True
            ).astype(jnp.int32)
            for d in range(3)
        ]
        corner_z[s] = jnp.broadcast_to(z, (patch_rows, BIN))
        x, y = x + which // 2, y + which % 2
        cells = jnp.where(y < cells_y, x * cells_y + y, own + cells_y + x)
        take[s] = (iota((patch_rows, 128), 1) == cells).astype(F32).astype(BF16)
        cells = jnp.sum(jnp.where(square, cells.astype(F32), 0.0), axis=0, keepdims=True)
        put[s] = (iota((128, patch_rows), 0).astype(F32) == cells).astype(F32).astype(BF16)

    far = iota((PZ, BIN), 0).astype(F32) * root

    def build_weights(s):
        def group(index, carry):
            at = pl.ds(pl.multiple_of(index * 8, 8), 8)
            scaled = fix[s, at, 2 * BIN : 3 * BIN] * ((PZ - 1.0) * root)
            totals = []
            for g in range(8):
                weight = jnp.exp2(-jnp.square(scaled[g : g + 1, :] - far))
                totals.append(jnp.sum(weight, axis=0, keepdims=True))
                those = pl.ds(pl.multiple_of(index * (8 * PZ) + g * PZ, PZ), PZ)
                high = weight.astype(BF16)
                w_high[those, :] = high
                w_low[those, :] = (weight - high.astype(F32)).astype(BF16)
            norms[at, :] = jnp.concatenate(totals, axis=0)
            return carry

        lax.fori_loop(0, bins // 8, group, 0)
        x_pair = pair_factor(fix[s, :, 0:BIN])
        y_pair = pair_factor(fix[s, :, BIN : 2 * BIN])
        norm = 1.0 / norms[...]
        for c in range(4):
            planar[c] = x_pair[c // 2] * (y_pair[c % 2] * norm)

    arrive(COUNT, 0, counts.at[1])
    fix[0] = merged(FIX_UP, FIX_DOWN, 0, fix_in, fix_out)
    send_fix(1, picked(turn[1], fix[0], 3))
    build_weights(0)
    loads["previous"].wait()

    lane = iota((8, 128), 1)
    bin_in_four = [2 * h + iota((8, 128), 0) // 4 for h in range(2)]
    nt = (((1,), (1,)), ((), ()))
    for s in range(STEPS):
        now = pressure if s == 0 else field.at[s - 1]
        before = previous if s == 0 else (pressure if s == 1 else field.at[s - 2])
        for kind in (X_HIGH, Y_HIGH, CORNER):
            arrive(kind, s, halo.at[s, kind])
        corner_row = jnp.where(iota((cells_y, depth), 0) == 0, halo[s, CORNER], 0.0)
        cells = jnp.concatenate(
            [
                now[...].reshape(own, depth),
                halo[s, X_HIGH],
                halo[s, Y_HIGH],
                corner_row,
                jnp.zeros((128 - own - 3 * cells_y, depth), F32),
            ],
            axis=0,
        )
        rows[...] = picked(take[s], cells, 2)
        rv[...] = merged(RV_UP, RV_DOWN, s, rv_in, rv_out)

        for q in range(bins // 4):
            halves = []
            for h in range(2):
                at = slice(16 * q + 8 * h, 16 * q + 8 * h + 8)
                z = corner_z[s, at, :] + lane % PZ
                found = [
                    jnp.take_along_axis(
                        rows[at, 128 * part : 128 * (part + 1)],
                        z % 128,
                        axis=1,
                        mode="promise_in_bounds",
                    )
                    for part in range(depth // 128)
                ]
                patch = jnp.where(z >= 128, found[1], found[0])
                halves.append(jnp.where(lane // PZ == bin_in_four[h], patch, 0.0))
            high, low = pieces(jnp.concatenate(halves, axis=0), 2)
            four = slice(128 * q, 128 * (q + 1))
            parts[16 * q : 16 * (q + 1), :] = (
                jnp.dot(high, w_high[four, :], preferred_element_type=F32)
                + jnp.dot(low, w_high[four, :], preferred_element_type=F32)
                + jnp.dot(high, w_low[four, :], preferred_element_type=F32)
            )
        outside = None
        for c in range(4):
            term = planar[c] * parts[pl.ds(c, bins, stride=4), :]
            outside = term if outside is None else outside + term
        r, v = rv[:, 0:BIN], rv[:, BIN : 2 * BIN]
        first_accel = wall_accel(r, v, outside)
        mid_r = r + 0.5 * time_step * v
        mid_v = v + 0.5 * time_step * first_accel
        second_accel = wall_accel(mid_r, mid_v, outside)
        fresh[:, 0:BIN] = r + time_step * mid_v
        fresh[:, BIN : 2 * BIN] = v + time_step * second_accel
        volume = four_pi * (2.0 * mid_r * mid_v * mid_v + mid_r * mid_r * second_accel)
        live = iota((bins, BIN), 1).astype(F32) < fix[s, :, 3 * BIN : 4 * BIN]
        volume = jnp.where(live, volume, 0.0)
        for c in range(4):
            shares[pl.ds(c, bins, stride=4), :] = planar[c] * volume
        for q in range(bins // 4):
            high, low = pieces(shares[16 * q : 16 * (q + 1), :], 2)
            four = slice(128 * q, 128 * (q + 1))
            given = (
                lax.dot_general(high, w_high[four, :], nt, preferred_element_type=F32)
                + lax.dot_general(low, w_high[four, :], nt, preferred_element_type=F32)
                + lax.dot_general(high, w_low[four, :], nt, preferred_element_type=F32)
            )
            for h in range(2):
                at = slice(16 * q + 8 * h, 16 * q + 8 * h + 8)
                for part in range(depth // 128):
                    away = lane + 128 * part - corner_z[s, at, :]
                    valid = (away >= 0) & (away < PZ)
                    found = jnp.take_along_axis(
                        given[8 * h : 8 * h + 8, :],
                        jnp.clip(away, 0, PZ - 1) + PZ * bin_in_four[h],
                        axis=1,
                        mode="promise_in_bounds",
                    )
                    placed[at, 128 * part : 128 * (part + 1)] = jnp.where(valid, found, 0.0)

        collected = picked(put[s], placed[...], 2)
        dep_out[s] = collected[own : own + 3 * cells_y, :]
        for part, kind in enumerate((DEP_X, DEP_Y, DEP_CORNER)):
            send(kind, s, dep_out.at[s, pl.ds(part * cells_y, cells_y)], dep_in.at[s, part])
        turned = picked(turn[s + 1], fresh[...], 3)
        if s + 1 < STEPS:
            send_rv(s + 1, turned)
        else:
            out_radius[...] = turned[:, :BIN]
            out_velocity[...] = turned[:, BIN:]
        if s + 1 < STEPS:
            fix[s + 1] = merged(FIX_UP, FIX_DOWN, s + 1, fix_in, fix_out)
            if s + 2 < STEPS:
                send_fix(s + 2, picked(turn[s + 2], fix[s + 1], 3))
            build_weights(s + 1)

        for kind in (X_LOW, Y_LOW):
            arrive(kind, s, halo.at[s, kind])
        after = out_pressure if s + 1 == STEPS else field.at[s]
        y_at, z_at = iota((cells_y, depth), 0), iota((cells_y, depth), 1)
        bases = []
        for x in range(cells_x):
            here = now[x]
            around = (halo[s, X_LOW] if x == 0 else now[x - 1]) + (
                halo[s, X_HIGH] if x == cells_x - 1 else now[x + 1]
            )
            around = around + jnp.where(
                y_at == 0, halo[s, Y_LOW, x : x + 1, :], pltpu.roll(here, 1, 0)
            )
            around = around + jnp.where(
                y_at == cells_y - 1, halo[s, Y_HIGH, x : x + 1, :], pltpu.roll(here, cells_y - 1, 0)
            )
            around = around + jnp.where(z_at == 0, 0.0, pltpu.roll(here, 1, 1))
            around = around + jnp.where(z_at == depth - 1, 0.0, pltpu.roll(here, depth - 1, 1))
            bases.append(
                2.0 * here
                - before[x]
                + courant_square * (around - 6.0 * here)
                + source_gain * collected[x * cells_y : (x + 1) * cells_y, :]
            )
        for part, kind in enumerate((DEP_X, DEP_Y, DEP_CORNER)):
            arrive(kind, s, dep_in.at[s, part])
        for x in range(cells_x):
            extra = jnp.where(y_at == 0, dep_in[s, 1, x : x + 1, :], 0.0)
            if x == 0:
                extra = extra + dep_in[s, 0] + dep_in[s, 2]
            after[x] = bases[x] + source_gain * extra
        if s + 1 < STEPS:
            send_halo(s + 1, after)

    for there, made in pending:

        @pl.when(there)
        def _():
            made.wait_send()


def local(
    slabs, bricks,
    pressure, previous, radius, velocity, positions, occupancy, anchors, migrations, crossings,
):
    cells_x, cells_y, depth = pressure.shape
    bins = radius.shape[0]
    most = bins // 2
    vmem = pl.BlockSpec(memory_space=pltpu.VMEM)
    hbm = pl.BlockSpec(memory_space=pltpu.HBM)
    scratch = [
        pltpu.VMEM(pressure.shape, F32),
        pltpu.VMEM(previous.shape, F32),
        pltpu.VMEM(radius.shape, F32),
        pltpu.VMEM(velocity.shape, F32),
        pltpu.VMEM(positions.shape, F32),
        pltpu.VMEM((1, bins), jnp.int32),
        pltpu.VMEM(anchors.shape, jnp.int32),
        pltpu.VMEM(migrations.shape, jnp.int32),
        pltpu.VMEM((1, STEPS), jnp.int32),
        pltpu.VMEM((STEPS, 5, cells_y, depth), F32),
        pltpu.VMEM((STEPS, 2, cells_y, depth), F32),
        pltpu.VMEM((STEPS, 3, cells_y, depth), F32),
        pltpu.VMEM((STEPS, 3 * cells_y, depth), F32),
        pltpu.VMEM((STEPS, 2, most, 4 * BIN), F32),
        pltpu.VMEM((STEPS, bins, 4 * BIN), F32),
        pltpu.VMEM((STEPS, bins, 4 * BIN), F32),
        pltpu.VMEM((STEPS, 2, most, 2 * BIN), F32),
        pltpu.VMEM((STEPS, bins, 2 * BIN), F32),
        pltpu.VMEM((bins, 2 * BIN), F32),
        pltpu.VMEM((2, 8, 128), jnp.int32),
        pltpu.VMEM((STEPS - 1, cells_x, cells_y, depth), F32),
        pltpu.VMEM((4 * bins, depth), F32),
        pltpu.VMEM((4 * bins, depth), F32),
        pltpu.VMEM((bins, 2 * BIN), F32),
        pltpu.VMEM((STEPS, 4 * bins, BIN), jnp.int32),
        pltpu.VMEM((STEPS, 4 * bins, 128), BF16),
        pltpu.VMEM((STEPS, 128, 4 * bins), BF16),
        pltpu.VMEM((STEPS + 1, bins, bins), BF16),
        pltpu.VMEM((4 * bins, BIN), F32),
        pltpu.VMEM((4 * bins, BIN), F32),
        pltpu.VMEM((4, bins, BIN), F32),
        pltpu.VMEM((bins, BIN), F32),
        pltpu.VMEM((PZ * bins, BIN), BF16),
        pltpu.VMEM((PZ * bins, BIN), BF16),
        pltpu.SemaphoreType.DMA((STEPS, KINDS)),
        pltpu.SemaphoreType.DMA((STEPS, KINDS)),
        pltpu.SemaphoreType.DMA((9,)),
    ]
    results = pl.pallas_call(
        functools.partial(kernel, slabs, bricks),
        out_shape=(
            jax.ShapeDtypeStruct(pressure.shape, F32),
            jax.ShapeDtypeStruct(radius.shape, F32),
            jax.ShapeDtypeStruct(velocity.shape, F32),
        ),
        in_specs=[hbm] * 9,
        out_specs=(vmem,) * 3,
        scratch_shapes=scratch,
        compiler_params=pltpu.CompilerParams(
            collective_id=0, has_side_effects=True, vmem_limit_bytes=60 * 1024 * 1024
        ),
    )(
        pressure, previous, radius, velocity, positions, occupancy.reshape(1, bins), anchors,
        migrations, crossings.reshape(1, STEPS),
    )
    return pl.pallas_call(
        handed_on,
        out_shape=tuple(jax.ShapeDtypeStruct(x.shape, F32) for x in results),
        in_specs=[hbm] * 3,
        out_specs=(hbm,) * 3,
        scratch_shapes=[pltpu.VMEM(x.shape, F32) for x in results]
        + [pltpu.SemaphoreType.DMA((2, 3))],
        compiler_params=pltpu.CompilerParams(vmem_limit_bytes=60 * 1024 * 1024),
    )(*results)


def handed_on(*refs):
    given, wanted, held, sem = refs[:3], refs[3:6], refs[6:9], refs[9]
    fetched = [pltpu.make_async_copy(given[i], held[i], sem.at[0, i]) for i in range(3)]
    stored = [pltpu.make_async_copy(held[i], wanted[i], sem.at[1, i]) for i in range(3)]
    for copy in fetched:
        copy.start()
    for i in range(3):
        fetched[i].wait()
        stored[i].start()
    for copy in stored:
        copy.wait()


def solution(mesh):
    placed = (
        P("slab", "brick", None),
        P("slab", "brick", None),
        P(("slab", "brick"), None),
        P(("slab", "brick"), None),
        P(None, ("slab", "brick"), None),
        P(("slab", "brick")),
        P(None, None, ("slab", "brick")),
        P(None, ("slab", "brick")),
        P(None, ("slab", "brick")),
    )
    return jax.shard_map(
        functools.partial(local, mesh.shape["slab"], mesh.shape["brick"]),
        mesh=mesh,
        in_specs=placed,
        out_specs=(
            P("slab", "brick", None),
            P(("slab", "brick"), None),
            P(("slab", "brick"), None),
        ),
        check_vma=False,
    )
```

```python
import functools

import jax
import jax.numpy as jnp
from jax import lax
from jax.experimental import pallas as pl
from jax.experimental.pallas import tpu as pltpu
from jax.sharding import PartitionSpec as P

BIN = 128
PZ = 32
STEPS = 3

courant_square = 0.25
source_gain = 0.05
kernel_width = 2.25
gas_pressure = 1.2
surface_tension = 0.1
viscosity = 0.02
polytropic = 1.4
sound_speed = 20.0
drive_gain = 0.5
time_step = 0.05
four_pi = 12.566370614359172
root = (1.4426950408889634 / (2.0 * kernel_width)) ** 0.5

MESH = pl.DeviceIdType.MESH
F32 = jnp.float32
BF16 = jnp.bfloat16

X_HIGH, X_LOW, Y_HIGH, Y_LOW, CORNER = range(5)
DEP_X, DEP_Y, DEP_CORNER = range(5, 8)
FIX_UP, FIX_DOWN, RV_UP, RV_DOWN, COUNT = range(8, 13)
OFFSETS = (
    (-1, 0), (1, 0), (0, -1), (0, 1), (-1, -1),
    (1, 0), (0, 1), (1, 1),
    (0, 1), (0, -1), (0, 1), (0, -1), (0, 1),
    (1, 0), (-1, 0), (0, 1), (0, -1), (1, 1), (-1, -1), (1, -1), (-1, 1),
)
MAIL = 13
MAIL_TILES = (3, 2, 3, 2, 3, 1, 1, 1)
KINDS = len(OFFSETS)


def pieces(value, count):
    found = []
    for _ in range(count - 1):
        piece = value.astype(BF16)
        found.append(piece)
        value = value - piece.astype(F32)
    found.append(value.astype(BF16))
    return found


def picked(one_hot, value, count):
    total = None
    for piece in pieces(value, count):
        term = jnp.dot(one_hot, piece, preferred_element_type=F32)
        total = term if total is None else total + term
    return total


def wall_accel(radius, velocity, outside):
    gas_term = gas_pressure * jnp.exp(-3.0 * polytropic * jnp.log(radius))
    inverse = 1.0 / radius
    wall_term = gas_term - (2.0 * surface_tension + 4.0 * viscosity * velocity) * inverse
    ambient = 1.0 + drive_gain * outside
    mach_number = velocity * (1.0 / sound_speed)
    driving = (1.0 + mach_number) * (wall_term - ambient) - 1.5 * (
        1.0 - mach_number * (1.0 / 3.0)
    ) * velocity * velocity
    return driving / ((1.0 - mach_number) * radius)


def iota(shape, dim):
    return lax.broadcasted_iota(jnp.int32, shape, dim)


def pair_factor(fraction):
    low = jnp.exp2(-jnp.square(fraction * root))
    high = jnp.exp2(-jnp.square((fraction - 1.0) * root))
    total = 1.0 / (low + high)
    return low * total, high * total


def kernel(
    slabs, bricks,
    pressure_hbm, previous_hbm, radius_hbm, velocity_hbm, positions_hbm, occupancy_hbm,
    anchors_hbm, migrations_hbm, crossings_hbm,
    out_pressure, out_radius, out_velocity,
    pressure, previous, radius, velocity, positions, occupancy, anchors, migrations, crossings,
    halo, edge, dep_in, dep_out, fix_in, fix_out, fix, rv_in, rv_out, rv, counts, field,
    rows, placed, fresh, corner_z, take, put, turn, parts, shares, planar, norms, w_high, w_low,
    mail_in, mail_out, partial, kept,
    send_sem, recv_sem, load_sem,
):
    loads = {}
    for index, (name, source, target) in enumerate(
        (
            ("migrations", migrations_hbm, migrations),
            ("radius", radius_hbm, radius),
            ("velocity", velocity_hbm, velocity),
            ("positions", positions_hbm, positions),
            ("occupancy", occupancy_hbm, occupancy),
            ("pressure", pressure_hbm, pressure),
            ("crossings", crossings_hbm, crossings),
            ("anchors", anchors_hbm, anchors),
            ("previous", previous_hbm, previous),
        )
    ):
        loads[name] = pltpu.make_async_copy(source, target, load_sem.at[index])
        loads[name].start()

    cells_x, cells_y, depth = pressure.shape
    bins = radius.shape[0]
    most = bins // 2
    own = cells_x * cells_y
    slab, brick = lax.axis_index("slab"), lax.axis_index("brick")

    def inside(dx, dy):
        a, b = slab + dx, brick + dy
        return (a >= 0) & (a < slabs) & (b >= 0) & (b < bricks)

    barrier = pltpu.get_barrier_semaphore()
    near = OFFSETS[MAIL:]
    expected = jnp.int32(0)
    for dx, dy in near:
        expected = expected + inside(dx, dy).astype(jnp.int32)

        @pl.when(inside(dx, dy))
        def _():
            pl.semaphore_signal(
                barrier, inc=1, device_id=(slab + dx, brick + dy), device_id_type=MESH
            )

    pending = []

    def copy(kind, step, source, target):
        dx, dy = OFFSETS[kind]
        return pltpu.make_async_remote_copy(
            src_ref=source,
            dst_ref=target,
            send_sem=send_sem.at[step, kind],
            recv_sem=recv_sem.at[step, kind],
            device_id=(slab + dx, brick + dy),
            device_id_type=MESH,
        )

    def send(kind, step, source, target):
        made = copy(kind, step, source, target)
        there = inside(*OFFSETS[kind])

        @pl.when(there)
        def _():
            made.start()

        pending.append((there, made))

    def arrive(kind, step, target):
        dx, dy = OFFSETS[kind]

        @pl.when(inside(-dx, -dy))
        def _():
            copy(kind, step, target, target).wait_recv()

    loads["migrations"].wait()
    eye = iota((bins, bins), 0) == iota((bins, bins), 1)

    def column(row):
        return jnp.sum(jnp.where(eye, jnp.broadcast_to(row, (bins, bins)), 0.0), axis=1, keepdims=True)

    slot_row = iota((1, bins), 1).astype(F32)
    slot_column = iota((bins, 1), 0).astype(F32)
    list_rows = [migrations[s : s + 1, :].astype(F32) for s in range(STEPS)]
    list_columns = [column(row) for row in list_rows]

    def turn_of(s):
        before = slot_row if s == 0 else list_rows[s - 1]
        after = slot_column if s == STEPS else list_columns[s]
        return (after == before).astype(F32).astype(BF16)

    def send_fix(s, value):
        fix_out[s] = value
        send(FIX_UP, s, fix_out.at[s, pl.ds(most, most)], fix_in.at[s, 0])
        send(FIX_DOWN, s, fix_out.at[s, pl.ds(0, most)], fix_in.at[s, 1])

    def send_rv(s, value):
        rv_out[s] = value
        send(RV_UP, s, rv_out.at[s, pl.ds(most, most)], rv_in.at[s, 0])
        send(RV_DOWN, s, rv_out.at[s, pl.ds(0, most)], rv_in.at[s, 1])

    def send_halo(s, block):
        edge[s, 0] = jnp.concatenate([block[x, 0:1, :] for x in range(cells_x)], axis=0)
        edge[s, 1] = jnp.concatenate(
            [block[x, cells_y - 1 : cells_y, :] for x in range(cells_x)], axis=0
        )
        send(X_HIGH, s, block.at[0], halo.at[s, X_HIGH])
        send(X_LOW, s, block.at[cells_x - 1], halo.at[s, X_LOW])
        send(Y_HIGH, s, edge.at[s, 0], halo.at[s, Y_HIGH])
        send(Y_LOW, s, edge.at[s, 1], halo.at[s, Y_LOW])
        send(CORNER, s, block.at[0], halo.at[s, CORNER])

    listed = iota((most, 1), 0)

    def merged(kind_up, kind_down, s, arrived, sent):
        arrive(kind_up, s, arrived.at[s, 0])
        arrive(kind_down, s, arrived.at[s, 1])
        width = sent.shape[2]
        from_below = jnp.broadcast_to(listed < counts[1, s : s + 1, 0:1], (most, width))
        from_above = jnp.broadcast_to(listed < counts[0, s : s + 1, 0:1], (most, width))
        return jnp.concatenate(
            [
                jnp.where(from_below, arrived[s, 0], sent[s, 0:most, :]),
                jnp.where(from_above, arrived[s, 1], sent[s, most:bins, :]),
            ],
            axis=0,
        )

    count_row = iota((8, 128), 0)

    for kind in range(5):
        dx, dy = OFFSETS[kind]

        @pl.when(jnp.logical_not(inside(-dx, -dy)))
        def _():
            halo[0, kind] = jnp.zeros((cells_y, depth), F32)

    for kind in (DEP_X, DEP_Y, DEP_CORNER):
        dx, dy = OFFSETS[kind]

        @pl.when(jnp.logical_not(inside(-dx, -dy)))
        def _():
            dep_in[STEPS - 1, kind - 5] = jnp.zeros((cells_y, depth), F32)

    for d in range(8):
        dx, dy = OFFSETS[MAIL + d]

        @pl.when(jnp.logical_not(inside(-dx, -dy)))
        def _():
            for s in range(STEPS - 1):
                mail_in[s, d] = jnp.zeros((3 * cells_y, depth), F32)

    @pl.when(brick == 0)
    def _():
        counts[1] = jnp.zeros((8, 128), jnp.int32)

    for name in ("radius", "velocity", "positions", "occupancy", "pressure", "crossings"):
        loads[name].wait()
    my_counts = jnp.zeros((8, 128), jnp.int32)
    for s in range(STEPS):
        my_counts = jnp.where(
            count_row == s, jnp.broadcast_to(crossings[:, s : s + 1], (8, 128)), my_counts
        )
    counts[0] = my_counts
    alive = jnp.broadcast_to(column(occupancy[...].astype(F32)), (bins, BIN))
    first = jnp.concatenate(
        [radius[...], velocity[...], positions[0], positions[1], positions[2], alive], axis=1
    )
    first = picked(turn_of(0), first, 3)

    pl.semaphore_wait(barrier, expected)
    counts_copy = copy(COUNT, 0, counts.at[0], counts.at[1])
    there = inside(*OFFSETS[COUNT])

    @pl.when(there)
    def _():
        counts_copy.start()

    pending.append((there, counts_copy))
    send_fix(0, first[:, 2 * BIN :])
    send_halo(0, pressure)
    send_rv(0, first[:, : 2 * BIN])

    loads["anchors"].wait()
    patch_rows = 4 * bins
    owner = iota((patch_rows, bins), 0) // 4 == iota((patch_rows, bins), 1)
    which = iota((patch_rows, 1), 0) % 4
    square = iota((patch_rows, patch_rows), 0) == iota((patch_rows, patch_rows), 1)
    for s in range(STEPS):
        turn[s + 1] = turn_of(s + 1)
        listed_slot = jnp.sum(jnp.where(owner, list_rows[s], 0.0), axis=1, keepdims=True)
        chosen = listed_slot == slot_row
        x, y, z = [
            jnp.sum(
                jnp.where(chosen, anchors[s, d : d + 1, :].astype(F32), 0.0), axis=1, keepdims=True
            ).astype(jnp.int32)
            for d in range(3)
        ]
        corner_z[s] = jnp.broadcast_to(z, (patch_rows, BIN))
        x, y = x + which // 2, y + which % 2
        cells = jnp.where(y < cells_y, x * cells_y + y, own + cells_y + x)
        take[s] = (iota((patch_rows, 128), 1) == cells).astype(F32).astype(BF16)
        cells = jnp.sum(jnp.where(square, cells.astype(F32), 0.0), axis=0, keepdims=True)
        put[s] = (iota((128, patch_rows), 0).astype(F32) == cells).astype(F32).astype(BF16)

    far = iota((PZ, BIN), 0).astype(F32) * root

    def build_weights(s):
        def group(index, carry):
            at = pl.ds(pl.multiple_of(index * 8, 8), 8)
            scaled = fix[s, at, 2 * BIN : 3 * BIN] * ((PZ - 1.0) * root)
            totals = []
            for g in range(8):
                weight = jnp.exp2(-jnp.square(scaled[g : g + 1, :] - far))
                totals.append(jnp.sum(weight, axis=0, keepdims=True))
                those = pl.ds(pl.multiple_of(index * (8 * PZ) + g * PZ, PZ), PZ)
                high = weight.astype(BF16)
                w_high[those, :] = high
                w_low[those, :] = (weight - high.astype(F32)).astype(BF16)
            norms[at, :] = jnp.concatenate(totals, axis=0)
            return carry

        lax.fori_loop(0, bins // 8, group, 0)
        x_pair = pair_factor(fix[s, :, 0:BIN])
        y_pair = pair_factor(fix[s, :, BIN : 2 * BIN])
        norm = 1.0 / norms[...]
        for c in range(4):
            planar[c] = x_pair[c // 2] * (y_pair[c % 2] * norm)

    arrive(COUNT, 0, counts.at[1])
    fix[0] = merged(FIX_UP, FIX_DOWN, 0, fix_in, fix_out)
    send_fix(1, picked(turn[1], fix[0], 3))
    build_weights(0)
    loads["previous"].wait()

    lane = iota((8, 128), 1)
    bin_in_four = [2 * h + iota((8, 128), 0) // 4 for h in range(2)]
    nt = (((1,), (1,)), ((), ()))
    for s in range(STEPS):
        now = pressure if s == 0 else field.at[s - 1]
        before = previous if s == 0 else (pressure if s == 1 else field.at[s - 2])
        if s == 0:
            for kind in range(5):
                arrive(kind, s, halo.at[s, kind])
        corner_row = jnp.where(iota((cells_y, depth), 0) == 0, halo[s, CORNER], 0.0)
        cells = jnp.concatenate(
            [
                now[...].reshape(own, depth),
                halo[s, X_HIGH],
                halo[s, Y_HIGH],
                corner_row,
                jnp.zeros((128 - own - 3 * cells_y, depth), F32),
            ],
            axis=0,
        )
        rows[...] = picked(take[s], cells, 2)
        rv[...] = merged(RV_UP, RV_DOWN, s, rv_in, rv_out)

        for q in range(bins // 4):
            halves = []
            for h in range(2):
                at = slice(16 * q + 8 * h, 16 * q + 8 * h + 8)
                z = corner_z[s, at, :] + lane % PZ
                found = [
                    jnp.take_along_axis(
                        rows[at, 128 * part : 128 * (part + 1)],
                        z % 128,
                        axis=1,
                        mode="promise_in_bounds",
                    )
                    for part in range(depth // 128)
                ]
                patch = jnp.where(z >= 128, found[1], found[0])
                halves.append(jnp.where(lane // PZ == bin_in_four[h], patch, 0.0))
            high, low = pieces(jnp.concatenate(halves, axis=0), 2)
            four = slice(128 * q, 128 * (q + 1))
            parts[16 * q : 16 * (q + 1), :] = (
                jnp.dot(high, w_high[four, :], preferred_element_type=F32)
                + jnp.dot(low, w_high[four, :], preferred_element_type=F32)
                + jnp.dot(high, w_low[four, :], preferred_element_type=F32)
            )
        outside = None
        for c in range(4):
            term = planar[c] * parts[pl.ds(c, bins, stride=4), :]
            outside = term if outside is None else outside + term
        r, v = rv[:, 0:BIN], rv[:, BIN : 2 * BIN]
        first_accel = wall_accel(r, v, outside)
        mid_r = r + 0.5 * time_step * v
        mid_v = v + 0.5 * time_step * first_accel
        second_accel = wall_accel(mid_r, mid_v, outside)
        fresh[:, 0:BIN] = r + time_step * mid_v
        fresh[:, BIN : 2 * BIN] = v + time_step * second_accel
        volume = four_pi * (2.0 * mid_r * mid_v * mid_v + mid_r * mid_r * second_accel)
        live = iota((bins, BIN), 1).astype(F32) < fix[s, :, 3 * BIN : 4 * BIN]
        volume = jnp.where(live, volume, 0.0)
        for c in range(4):
            shares[pl.ds(c, bins, stride=4), :] = planar[c] * volume
        for q in range(bins // 4):
            high, low = pieces(shares[16 * q : 16 * (q + 1), :], 2)
            four = slice(128 * q, 128 * (q + 1))
            given = (
                lax.dot_general(high, w_high[four, :], nt, preferred_element_type=F32)
                + lax.dot_general(low, w_high[four, :], nt, preferred_element_type=F32)
                + lax.dot_general(high, w_low[four, :], nt, preferred_element_type=F32)
            )
            for h in range(2):
                at = slice(16 * q + 8 * h, 16 * q + 8 * h + 8)
                for part in range(depth // 128):
                    away = lane + 128 * part - corner_z[s, at, :]
                    valid = (away >= 0) & (away < PZ)
                    found = jnp.take_along_axis(
                        given[8 * h : 8 * h + 8, :],
                        jnp.clip(away, 0, PZ - 1) + PZ * bin_in_four[h],
                        axis=1,
                        mode="promise_in_bounds",
                    )
                    placed[at, 128 * part : 128 * (part + 1)] = jnp.where(valid, found, 0.0)

        collected = picked(put[s], placed[...], 2)
        x_face, y_face, corner_face = [
            source_gain * collected[own + part * cells_y : own + (part + 1) * cells_y, :]
            for part in range(3)
        ]
        if s + 1 == STEPS:
            for part, face in enumerate((x_face, y_face, corner_face)):
                dep_out[s, part * cells_y : (part + 1) * cells_y, :] = face
            for part, kind in enumerate((DEP_X, DEP_Y, DEP_CORNER)):
                send(kind, s, dep_out.at[s, pl.ds(part * cells_y, cells_y)], dep_in.at[s, part])
        after = out_pressure if s + 1 == STEPS else field.at[s]
        y_at, z_at = iota((cells_y, depth), 0), iota((cells_y, depth), 1)
        bases = []
        for x in range(cells_x):
            here = now[x]
            around = (halo[s, X_LOW] if x == 0 else now[x - 1]) + (
                halo[s, X_HIGH] if x == cells_x - 1 else now[x + 1]
            )
            around = around + jnp.where(
                y_at == 0, halo[s, Y_LOW, x : x + 1, :], pltpu.roll(here, 1, 0)
            )
            around = around + jnp.where(
                y_at == cells_y - 1, halo[s, Y_HIGH, x : x + 1, :], pltpu.roll(here, cells_y - 1, 0)
            )
            around = around + jnp.where(z_at == 0, 0.0, pltpu.roll(here, 1, 1))
            around = around + jnp.where(z_at == depth - 1, 0.0, pltpu.roll(here, depth - 1, 1))
            bases.append(
                2.0 * here
                - before[x]
                + courant_square * (around - 6.0 * here)
                + source_gain * collected[x * cells_y : (x + 1) * cells_y, :]
            )
        if s + 1 < STEPS:
            y_first = jnp.concatenate([base[0:1, :] for base in bases], axis=0)
            y_last = jnp.concatenate([base[cells_y - 1 :, :] for base in bases], axis=0)
            mails = (
                (x_face, bases[cells_x - 1], corner_face),
                (bases[0], y_face),
                (y_face, y_last, corner_face),
                (y_first, x_face),
                (corner_face, y_face, x_face),
                (bases[0],),
                (x_face,),
                (y_face,),
            )
            for d, mail in enumerate(mails):
                for part, tile in enumerate(mail):
                    mail_out[s, d, part * cells_y : (part + 1) * cells_y, :] = tile
            for d in range(8):
                size = pl.ds(0, MAIL_TILES[d] * cells_y)
                send(MAIL + d, s, mail_out.at[s, d, size], mail_in.at[s, d, size])
        for x in range(cells_x):
            partial[x] = bases[x]
        if s + 1 < STEPS:
            kept[0], kept[1], kept[2] = x_face, y_face, corner_face
        turned = picked(turn[s + 1], fresh[...], 3)
        if s + 1 < STEPS:
            send_rv(s + 1, turned)
        else:
            out_radius[...] = turned[:, :BIN]
            out_velocity[...] = turned[:, BIN:]
        if s + 1 < STEPS:
            fix[s + 1] = merged(FIX_UP, FIX_DOWN, s + 1, fix_in, fix_out)
            if s + 2 < STEPS:
                send_fix(s + 2, picked(turn[s + 2], fix[s + 1], 3))
            build_weights(s + 1)

        first_row = y_at == 0

        def tile(d, part):
            return mail_in[s, d, part * cells_y : (part + 1) * cells_y, :]

        if s + 1 == STEPS:
            for part, kind in enumerate((DEP_X, DEP_Y, DEP_CORNER)):
                arrive(kind, s, dep_in.at[s, part])
            at_x, at_y, at_corner = [dep_in[s, part] for part in range(3)]
        else:
            for d in range(8):
                arrive(MAIL + d, s, mail_in.at[s, d, pl.ds(0, MAIL_TILES[d] * cells_y)])
            at_x, at_y, at_corner = tile(0, 0), tile(2, 0), tile(4, 0)

            def at_first(value):
                return jnp.where(first_row, value, 0.0)

            last_x = mail_in[s, 4, 2 * cells_y - 1 : 2 * cells_y, :]
            last_y = mail_in[s, 4, 3 * cells_y - 1 : 3 * cells_y, :]
            x_high = tile(1, 0) + kept[0] + at_first(tile(2, 2) + tile(7, 0))
            y_high = tile(3, 0) + kept[1] + at_first(tile(0, 2) + tile(6, 0))
            corner = tile(5, 0) + kept[2] + tile(1, 1) + tile(3, 1)
            halo[s + 1, X_HIGH] = jnp.where(inside(1, 0), x_high, 0.0)
            halo[s + 1, Y_HIGH] = jnp.where(inside(0, 1), y_high, 0.0)
            halo[s + 1, CORNER] = jnp.where(inside(1, 1), corner, 0.0)
            halo[s + 1, X_LOW] = tile(0, 1) + at_first(last_x)
            halo[s + 1, Y_LOW] = tile(2, 1) + at_first(last_y)
        for x in range(cells_x):
            extra = jnp.where(first_row, at_y[x : x + 1, :], 0.0)
            if x == 0:
                extra = extra + at_x + at_corner
            after[x] = partial[x] + extra

    for there, made in pending:

        @pl.when(there)
        def _():
            made.wait_send()


def local(
    slabs, bricks,
    pressure, previous, radius, velocity, positions, occupancy, anchors, migrations, crossings,
):
    cells_x, cells_y, depth = pressure.shape
    bins = radius.shape[0]
    most = bins // 2
    vmem = pl.BlockSpec(memory_space=pltpu.VMEM)
    hbm = pl.BlockSpec(memory_space=pltpu.HBM)
    scratch = [
        pltpu.VMEM(pressure.shape, F32),
        pltpu.VMEM(previous.shape, F32),
        pltpu.VMEM(radius.shape, F32),
        pltpu.VMEM(velocity.shape, F32),
        pltpu.VMEM(positions.shape, F32),
        pltpu.VMEM((1, bins), jnp.int32),
        pltpu.VMEM(anchors.shape, jnp.int32),
        pltpu.VMEM(migrations.shape, jnp.int32),
        pltpu.VMEM((1, STEPS), jnp.int32),
        pltpu.VMEM((STEPS, 5, cells_y, depth), F32),
        pltpu.VMEM((STEPS, 2, cells_y, depth), F32),
        pltpu.VMEM((STEPS, 3, cells_y, depth), F32),
        pltpu.VMEM((STEPS, 3 * cells_y, depth), F32),
        pltpu.VMEM((STEPS, 2, most, 4 * BIN), F32),
        pltpu.VMEM((STEPS, bins, 4 * BIN), F32),
        pltpu.VMEM((STEPS, bins, 4 * BIN), F32),
        pltpu.VMEM((STEPS, 2, most, 2 * BIN), F32),
        pltpu.VMEM((STEPS, bins, 2 * BIN), F32),
        pltpu.VMEM((bins, 2 * BIN), F32),
        pltpu.VMEM((2, 8, 128), jnp.int32),
        pltpu.VMEM((STEPS - 1, cells_x, cells_y, depth), F32),
        pltpu.VMEM((4 * bins, depth), F32),
        pltpu.VMEM((4 * bins, depth), F32),
        pltpu.VMEM((bins, 2 * BIN), F32),
        pltpu.VMEM((STEPS, 4 * bins, BIN), jnp.int32),
        pltpu.VMEM((STEPS, 4 * bins, 128), BF16),
        pltpu.VMEM((STEPS, 128, 4 * bins), BF16),
        pltpu.VMEM((STEPS + 1, bins, bins), BF16),
        pltpu.VMEM((4 * bins, BIN), F32),
        pltpu.VMEM((4 * bins, BIN), F32),
        pltpu.VMEM((4, bins, BIN), F32),
        pltpu.VMEM((bins, BIN), F32),
        pltpu.VMEM((PZ * bins, BIN), BF16),
        pltpu.VMEM((PZ * bins, BIN), BF16),
        pltpu.VMEM((STEPS - 1, 8, 3 * cells_y, depth), F32),
        pltpu.VMEM((STEPS - 1, 8, 3 * cells_y, depth), F32),
        pltpu.VMEM(pressure.shape, F32),
        pltpu.VMEM((3, cells_y, depth), F32),
        pltpu.SemaphoreType.DMA((STEPS, KINDS)),
        pltpu.SemaphoreType.DMA((STEPS, KINDS)),
        pltpu.SemaphoreType.DMA((9,)),
    ]
    results = pl.pallas_call(
        functools.partial(kernel, slabs, bricks),
        out_shape=(
            jax.ShapeDtypeStruct(pressure.shape, F32),
            jax.ShapeDtypeStruct(radius.shape, F32),
            jax.ShapeDtypeStruct(velocity.shape, F32),
        ),
        in_specs=[hbm] * 9,
        out_specs=(vmem,) * 3,
        scratch_shapes=scratch,
        compiler_params=pltpu.CompilerParams(
            collective_id=0, has_side_effects=True, vmem_limit_bytes=60 * 1024 * 1024
        ),
    )(
        pressure, previous, radius, velocity, positions, occupancy.reshape(1, bins), anchors,
        migrations, crossings.reshape(1, STEPS),
    )
    return pl.pallas_call(
        handed_on,
        out_shape=tuple(jax.ShapeDtypeStruct(x.shape, F32) for x in results),
        in_specs=[hbm] * 3,
        out_specs=(hbm,) * 3,
        scratch_shapes=[pltpu.VMEM(x.shape, F32) for x in results]
        + [pltpu.SemaphoreType.DMA((2, 3))],
        compiler_params=pltpu.CompilerParams(vmem_limit_bytes=60 * 1024 * 1024),
    )(*results)


def handed_on(*refs):
    given, wanted, held, sem = refs[:3], refs[3:6], refs[6:9], refs[9]
    fetched = [pltpu.make_async_copy(given[i], held[i], sem.at[0, i]) for i in range(3)]
    stored = [pltpu.make_async_copy(held[i], wanted[i], sem.at[1, i]) for i in range(3)]
    for copy in fetched:
        copy.start()
    for i in range(3):
        fetched[i].wait()
        stored[i].start()
    for copy in stored:
        copy.wait()


def solution(mesh):
    placed = (
        P("slab", "brick", None),
        P("slab", "brick", None),
        P(("slab", "brick"), None),
        P(("slab", "brick"), None),
        P(None, ("slab", "brick"), None),
        P(("slab", "brick")),
        P(None, None, ("slab", "brick")),
        P(None, ("slab", "brick")),
        P(None, ("slab", "brick")),
    )
    return jax.shard_map(
        functools.partial(local, mesh.shape["slab"], mesh.shape["brick"]),
        mesh=mesh,
        in_specs=placed,
        out_specs=(
            P("slab", "brick", None),
            P(("slab", "brick"), None),
            P(("slab", "brick"), None),
        ),
        check_vma=False,
    )
```

```python
import functools

import jax
import jax.numpy as jnp
from jax import lax
from jax.experimental import pallas as pl
from jax.experimental.pallas import tpu as pltpu
from jax.sharding import PartitionSpec as P

BIN = 128
PZ = 32
STEPS = 3

courant_square = 0.25
source_gain = 0.05
kernel_width = 2.25
gas_pressure = 1.2
surface_tension = 0.1
viscosity = 0.02
polytropic = 1.4
sound_speed = 20.0
drive_gain = 0.5
time_step = 0.05
four_pi = 12.566370614359172
root = (1.4426950408889634 / (2.0 * kernel_width)) ** 0.5

MESH = pl.DeviceIdType.MESH
F32 = jnp.float32
BF16 = jnp.bfloat16

X_HIGH, X_LOW, Y_HIGH, Y_LOW, CORNER = range(5)
DEP_X, DEP_Y, DEP_CORNER = range(5, 8)
FIX_UP, FIX_DOWN, RV_UP, RV_DOWN, COUNT = range(8, 13)
OFFSETS = (
    (-1, 0), (1, 0), (0, -1), (0, 1), (-1, -1),
    (1, 0), (0, 1), (1, 1),
    (0, 1), (0, -1), (0, 1), (0, -1), (0, 1),
    (1, 0), (-1, 0), (0, 1), (0, -1), (1, 1), (-1, -1), (1, -1), (-1, 1),
)
MAIL = 13
MAIL_TILES = (3, 2, 3, 2, 3, 1, 1, 1)
KINDS = len(OFFSETS)


def pieces(value, count):
    found = []
    for _ in range(count - 1):
        piece = value.astype(BF16)
        found.append(piece)
        value = value - piece.astype(F32)
    found.append(value.astype(BF16))
    return found


def picked(one_hot, value, count):
    total = None
    for piece in pieces(value, count):
        term = jnp.dot(one_hot, piece, preferred_element_type=F32)
        total = term if total is None else total + term
    return total


def wall_accel(radius, velocity, outside):
    gas_term = gas_pressure * jnp.exp(-3.0 * polytropic * jnp.log(radius))
    inverse = 1.0 / radius
    wall_term = gas_term - (2.0 * surface_tension + 4.0 * viscosity * velocity) * inverse
    ambient = 1.0 + drive_gain * outside
    mach_number = velocity * (1.0 / sound_speed)
    driving = (1.0 + mach_number) * (wall_term - ambient) - 1.5 * (
        1.0 - mach_number * (1.0 / 3.0)
    ) * velocity * velocity
    return driving / ((1.0 - mach_number) * radius)


def iota(shape, dim):
    return lax.broadcasted_iota(jnp.int32, shape, dim)


def pair_factor(fraction):
    low = jnp.exp2(-jnp.square(fraction * root))
    high = jnp.exp2(-jnp.square((fraction - 1.0) * root))
    total = 1.0 / (low + high)
    return low * total, high * total


def kernel(
    slabs, bricks,
    pressure_hbm, previous_hbm, radius_hbm, velocity_hbm, positions_hbm, occupancy_hbm,
    anchors_hbm, migrations_hbm, crossings_hbm,
    out_pressure, out_radius, out_velocity,
    pressure, previous, radius, velocity, positions, occupancy, anchors, migrations, crossings,
    halo, edge, dep_in, dep_out, fix_in, fix_out, fix, rv_in, rv_out, rv, counts, field,
    rows, placed, fresh, corner_z, take, put, turn, parts, shares, planar, norms, w_high, w_low,
    mail_in, mail_out, partial, kept,
    send_sem, recv_sem, load_sem,
):
    loads = {}
    for index, (name, source, target) in enumerate(
        (
            ("migrations", migrations_hbm, migrations),
            ("radius", radius_hbm, radius),
            ("velocity", velocity_hbm, velocity),
            ("positions", positions_hbm, positions),
            ("occupancy", occupancy_hbm, occupancy),
            ("pressure", pressure_hbm, pressure),
            ("crossings", crossings_hbm, crossings),
            ("anchors", anchors_hbm, anchors),
            ("previous", previous_hbm, previous),
        )
    ):
        loads[name] = pltpu.make_async_copy(source, target, load_sem.at[index])
        loads[name].start()

    cells_x, cells_y, depth = pressure.shape
    bins = radius.shape[0]
    most = bins // 2
    own = cells_x * cells_y
    slab, brick = lax.axis_index("slab"), lax.axis_index("brick")

    def inside(dx, dy):
        a, b = slab + dx, brick + dy
        return (a >= 0) & (a < slabs) & (b >= 0) & (b < bricks)

    barrier = pltpu.get_barrier_semaphore()
    near = OFFSETS[MAIL:]
    expected = jnp.int32(0)
    for dx, dy in near:
        expected = expected + inside(dx, dy).astype(jnp.int32)

        @pl.when(inside(dx, dy))
        def _():
            pl.semaphore_signal(
                barrier, inc=1, device_id=(slab + dx, brick + dy), device_id_type=MESH
            )

    pending = []

    def copy(kind, step, source, target):
        dx, dy = OFFSETS[kind]
        return pltpu.make_async_remote_copy(
            src_ref=source,
            dst_ref=target,
            send_sem=send_sem.at[step, kind],
            recv_sem=recv_sem.at[step, kind],
            device_id=(slab + dx, brick + dy),
            device_id_type=MESH,
        )

    def send(kind, step, source, target):
        made = copy(kind, step, source, target)
        there = inside(*OFFSETS[kind])

        @pl.when(there)
        def _():
            made.start()

        pending.append((there, made))

    def arrive(kind, step, target):
        dx, dy = OFFSETS[kind]

        @pl.when(inside(-dx, -dy))
        def _():
            copy(kind, step, target, target).wait_recv()

    loads["migrations"].wait()
    eye = iota((bins, bins), 0) == iota((bins, bins), 1)

    def column(row):
        return jnp.sum(jnp.where(eye, jnp.broadcast_to(row, (bins, bins)), 0.0), axis=1, keepdims=True)

    slot_row = iota((1, bins), 1).astype(F32)
    slot_column = iota((bins, 1), 0).astype(F32)
    list_rows = [migrations[s : s + 1, :].astype(F32) for s in range(STEPS)]
    list_columns = [column(row) for row in list_rows]

    def turn_of(s):
        before = slot_row if s == 0 else list_rows[s - 1]
        after = slot_column if s == STEPS else list_columns[s]
        return (after == before).astype(F32).astype(BF16)

    def send_fix(s, value):
        fix_out[s] = value
        send(FIX_UP, s, fix_out.at[s, pl.ds(most, most)], fix_in.at[s, 0])
        send(FIX_DOWN, s, fix_out.at[s, pl.ds(0, most)], fix_in.at[s, 1])

    def send_rv(s, value):
        rv_out[s] = value
        send(RV_UP, s, rv_out.at[s, pl.ds(most, most)], rv_in.at[s, 0])
        send(RV_DOWN, s, rv_out.at[s, pl.ds(0, most)], rv_in.at[s, 1])

    def send_halo(s, block):
        edge[s, 0] = jnp.concatenate([block[x, 0:1, :] for x in range(cells_x)], axis=0)
        edge[s, 1] = jnp.concatenate(
            [block[x, cells_y - 1 : cells_y, :] for x in range(cells_x)], axis=0
        )
        send(X_HIGH, s, block.at[0], halo.at[s, X_HIGH])
        send(X_LOW, s, block.at[cells_x - 1], halo.at[s, X_LOW])
        send(Y_HIGH, s, edge.at[s, 0], halo.at[s, Y_HIGH])
        send(Y_LOW, s, edge.at[s, 1], halo.at[s, Y_LOW])
        send(CORNER, s, block.at[0], halo.at[s, CORNER])

    listed = iota((most, 1), 0)

    def merged(kind_up, kind_down, s, arrived, sent):
        arrive(kind_up, s, arrived.at[s, 0])
        arrive(kind_down, s, arrived.at[s, 1])
        width = sent.shape[2]
        from_below = jnp.broadcast_to(listed < counts[1, s : s + 1, 0:1], (most, width))
        from_above = jnp.broadcast_to(listed < counts[0, s : s + 1, 0:1], (most, width))
        return jnp.concatenate(
            [
                jnp.where(from_below, arrived[s, 0], sent[s, 0:most, :]),
                jnp.where(from_above, arrived[s, 1], sent[s, most:bins, :]),
            ],
            axis=0,
        )

    count_row = iota((8, 128), 0)

    for kind in range(5):
        dx, dy = OFFSETS[kind]

        @pl.when(jnp.logical_not(inside(-dx, -dy)))
        def _():
            halo[0, kind] = jnp.zeros((cells_y, depth), F32)

    for kind in (DEP_X, DEP_Y, DEP_CORNER):
        dx, dy = OFFSETS[kind]

        @pl.when(jnp.logical_not(inside(-dx, -dy)))
        def _():
            dep_in[STEPS - 1, kind - 5] = jnp.zeros((cells_y, depth), F32)

    for d in range(8):
        dx, dy = OFFSETS[MAIL + d]

        @pl.when(jnp.logical_not(inside(-dx, -dy)))
        def _():
            for s in range(STEPS - 1):
                mail_in[s, d] = jnp.zeros((3 * cells_y, depth), F32)

    @pl.when(brick == 0)
    def _():
        counts[1] = jnp.zeros((8, 128), jnp.int32)

    for name in ("radius", "velocity", "positions", "occupancy", "pressure", "crossings"):
        loads[name].wait()
    my_counts = jnp.zeros((8, 128), jnp.int32)
    for s in range(STEPS):
        my_counts = jnp.where(
            count_row == s, jnp.broadcast_to(crossings[:, s : s + 1], (8, 128)), my_counts
        )
    counts[0] = my_counts
    alive = jnp.broadcast_to(column(occupancy[...].astype(F32)), (bins, BIN))
    first = jnp.concatenate(
        [radius[...], velocity[...], positions[0], positions[1], positions[2], alive], axis=1
    )
    first = picked(turn_of(0), first, 3)

    pl.semaphore_wait(barrier, expected)
    counts_copy = copy(COUNT, 0, counts.at[0], counts.at[1])
    there = inside(*OFFSETS[COUNT])

    @pl.when(there)
    def _():
        counts_copy.start()

    pending.append((there, counts_copy))
    send_fix(0, first[:, 2 * BIN :])
    send_halo(0, pressure)
    send_rv(0, first[:, : 2 * BIN])

    loads["anchors"].wait()
    patch_rows = 4 * bins
    owner = iota((patch_rows, bins), 0) // 4 == iota((patch_rows, bins), 1)
    which = iota((patch_rows, 1), 0) % 4
    square = iota((patch_rows, patch_rows), 0) == iota((patch_rows, patch_rows), 1)
    for s in range(STEPS):
        turn[s + 1] = turn_of(s + 1)

    def build_corners(s):
        listed_slot = jnp.sum(jnp.where(owner, list_rows[s], 0.0), axis=1, keepdims=True)
        chosen = listed_slot == slot_row
        x, y, z = [
            jnp.sum(
                jnp.where(chosen, anchors[s, d : d + 1, :].astype(F32), 0.0), axis=1, keepdims=True
            ).astype(jnp.int32)
            for d in range(3)
        ]
        corner_z[s] = jnp.broadcast_to(z, (patch_rows, BIN))
        x, y = x + which // 2, y + which % 2
        cells = jnp.where(y < cells_y, x * cells_y + y, own + cells_y + x)
        take[s] = (iota((patch_rows, 128), 1) == cells).astype(F32).astype(BF16)
        cells = jnp.sum(jnp.where(square, cells.astype(F32), 0.0), axis=0, keepdims=True)
        put[s] = (iota((128, patch_rows), 0).astype(F32) == cells).astype(F32).astype(BF16)

    far = iota((PZ, BIN), 0).astype(F32) * root

    def build_weights(s):
        def group(index, carry):
            at = pl.ds(pl.multiple_of(index * 8, 8), 8)
            scaled = fix[s, at, 2 * BIN : 3 * BIN] * ((PZ - 1.0) * root)
            totals = []
            for g in range(8):
                weight = jnp.exp2(-jnp.square(scaled[g : g + 1, :] - far))
                totals.append(jnp.sum(weight, axis=0, keepdims=True))
                those = pl.ds(pl.multiple_of(index * (8 * PZ) + g * PZ, PZ), PZ)
                high = weight.astype(BF16)
                w_high[those, :] = high
                w_low[those, :] = (weight - high.astype(F32)).astype(BF16)
            norms[at, :] = jnp.concatenate(totals, axis=0)
            return carry

        lax.fori_loop(0, bins // 8, group, 0)
        x_pair = pair_factor(fix[s, :, 0:BIN])
        y_pair = pair_factor(fix[s, :, BIN : 2 * BIN])
        norm = 1.0 / norms[...]
        for c in range(4):
            planar[c] = x_pair[c // 2] * (y_pair[c % 2] * norm)

    arrive(COUNT, 0, counts.at[1])
    fix[0] = merged(FIX_UP, FIX_DOWN, 0, fix_in, fix_out)
    send_fix(1, picked(turn[1], fix[0], 3))
    build_weights(0)
    build_corners(0)
    loads["previous"].wait()

    lane = iota((8, 128), 1)
    bin_in_four = [2 * h + iota((8, 128), 0) // 4 for h in range(2)]
    nt = (((1,), (1,)), ((), ()))
    for s in range(STEPS):
        now = pressure if s == 0 else field.at[s - 1]
        before = previous if s == 0 else (pressure if s == 1 else field.at[s - 2])
        if s == 0:
            for kind in range(5):
                arrive(kind, s, halo.at[s, kind])
        corner_row = jnp.where(iota((cells_y, depth), 0) == 0, halo[s, CORNER], 0.0)
        cells = jnp.concatenate(
            [
                now[...].reshape(own, depth),
                halo[s, X_HIGH],
                halo[s, Y_HIGH],
                corner_row,
                jnp.zeros((128 - own - 3 * cells_y, depth), F32),
            ],
            axis=0,
        )
        rows[...] = picked(take[s], cells, 2)
        rv[...] = merged(RV_UP, RV_DOWN, s, rv_in, rv_out)

        for q in range(bins // 4):
            halves = []
            for h in range(2):
                at = slice(16 * q + 8 * h, 16 * q + 8 * h + 8)
                z = corner_z[s, at, :] + lane % PZ
                found = [
                    jnp.take_along_axis(
                        rows[at, 128 * part : 128 * (part + 1)],
                        z % 128,
                        axis=1,
                        mode="promise_in_bounds",
                    )
                    for part in range(depth // 128)
                ]
                patch = jnp.where(z >= 128, found[1], found[0])
                halves.append(jnp.where(lane // PZ == bin_in_four[h], patch, 0.0))
            high, low = pieces(jnp.concatenate(halves, axis=0), 2)
            four = slice(128 * q, 128 * (q + 1))
            parts[16 * q : 16 * (q + 1), :] = (
                jnp.dot(high, w_high[four, :], preferred_element_type=F32)
                + jnp.dot(low, w_high[four, :], preferred_element_type=F32)
                + jnp.dot(high, w_low[four, :], preferred_element_type=F32)
            )
        outside = None
        for c in range(4):
            term = planar[c] * parts[pl.ds(c, bins, stride=4), :]
            outside = term if outside is None else outside + term
        r, v = rv[:, 0:BIN], rv[:, BIN : 2 * BIN]
        first_accel = wall_accel(r, v, outside)
        mid_r = r + 0.5 * time_step * v
        mid_v = v + 0.5 * time_step * first_accel
        second_accel = wall_accel(mid_r, mid_v, outside)
        fresh[:, 0:BIN] = r + time_step * mid_v
        fresh[:, BIN : 2 * BIN] = v + time_step * second_accel
        volume = four_pi * (2.0 * mid_r * mid_v * mid_v + mid_r * mid_r * second_accel)
        live = iota((bins, BIN), 1).astype(F32) < fix[s, :, 3 * BIN : 4 * BIN]
        volume = jnp.where(live, volume, 0.0)
        for c in range(4):
            shares[pl.ds(c, bins, stride=4), :] = planar[c] * volume
        for q in range(bins // 4):
            high, low = pieces(shares[16 * q : 16 * (q + 1), :], 2)
            four = slice(128 * q, 128 * (q + 1))
            given = (
                lax.dot_general(high, w_high[four, :], nt, preferred_element_type=F32)
                + lax.dot_general(low, w_high[four, :], nt, preferred_element_type=F32)
                + lax.dot_general(high, w_low[four, :], nt, preferred_element_type=F32)
            )
            for h in range(2):
                at = slice(16 * q + 8 * h, 16 * q + 8 * h + 8)
                for part in range(depth // 128):
                    away = lane + 128 * part - corner_z[s, at, :]
                    valid = (away >= 0) & (away < PZ)
                    found = jnp.take_along_axis(
                        given[8 * h : 8 * h + 8, :],
                        jnp.clip(away, 0, PZ - 1) + PZ * bin_in_four[h],
                        axis=1,
                        mode="promise_in_bounds",
                    )
                    placed[at, 128 * part : 128 * (part + 1)] = jnp.where(valid, found, 0.0)

        collected = picked(put[s], placed[...], 2)
        x_face, y_face, corner_face = [
            source_gain * collected[own + part * cells_y : own + (part + 1) * cells_y, :]
            for part in range(3)
        ]
        if s + 1 == STEPS:
            for part, face in enumerate((x_face, y_face, corner_face)):
                dep_out[s, part * cells_y : (part + 1) * cells_y, :] = face
            for part, kind in enumerate((DEP_X, DEP_Y, DEP_CORNER)):
                send(kind, s, dep_out.at[s, pl.ds(part * cells_y, cells_y)], dep_in.at[s, part])
        after = out_pressure if s + 1 == STEPS else field.at[s]
        y_at, z_at = iota((cells_y, depth), 0), iota((cells_y, depth), 1)
        bases = []
        for x in range(cells_x):
            here = now[x]
            around = (halo[s, X_LOW] if x == 0 else now[x - 1]) + (
                halo[s, X_HIGH] if x == cells_x - 1 else now[x + 1]
            )
            around = around + jnp.where(
                y_at == 0, halo[s, Y_LOW, x : x + 1, :], pltpu.roll(here, 1, 0)
            )
            around = around + jnp.where(
                y_at == cells_y - 1, halo[s, Y_HIGH, x : x + 1, :], pltpu.roll(here, cells_y - 1, 0)
            )
            around = around + jnp.where(z_at == 0, 0.0, pltpu.roll(here, 1, 1))
            around = around + jnp.where(z_at == depth - 1, 0.0, pltpu.roll(here, depth - 1, 1))
            bases.append(
                2.0 * here
                - before[x]
                + courant_square * (around - 6.0 * here)
                + source_gain * collected[x * cells_y : (x + 1) * cells_y, :]
            )
        if s + 1 < STEPS:
            y_first = jnp.concatenate([base[0:1, :] for base in bases], axis=0)
            y_last = jnp.concatenate([base[cells_y - 1 :, :] for base in bases], axis=0)
            mails = (
                (x_face, bases[cells_x - 1], corner_face),
                (bases[0], y_face),
                (y_face, y_last, corner_face),
                (y_first, x_face),
                (corner_face, y_face, x_face),
                (bases[0],),
                (x_face,),
                (y_face,),
            )
            for d, mail in enumerate(mails):
                for part, tile in enumerate(mail):
                    mail_out[s, d, part * cells_y : (part + 1) * cells_y, :] = tile
            for d in range(8):
                size = pl.ds(0, MAIL_TILES[d] * cells_y)
                send(MAIL + d, s, mail_out.at[s, d, size], mail_in.at[s, d, size])
        for x in range(cells_x):
            partial[x] = bases[x]
        if s + 1 < STEPS:
            kept[0], kept[1], kept[2] = x_face, y_face, corner_face
        turned = picked(turn[s + 1], fresh[...], 3)
        if s + 1 < STEPS:
            send_rv(s + 1, turned)
        else:
            out_radius[...] = turned[:, :BIN]
            out_velocity[...] = turned[:, BIN:]
        if s + 1 < STEPS:
            fix[s + 1] = merged(FIX_UP, FIX_DOWN, s + 1, fix_in, fix_out)
            if s + 2 < STEPS:
                send_fix(s + 2, picked(turn[s + 2], fix[s + 1], 3))
            build_weights(s + 1)
            build_corners(s + 1)

        first_row = y_at == 0

        def tile(d, part):
            return mail_in[s, d, part * cells_y : (part + 1) * cells_y, :]

        if s + 1 == STEPS:
            for part, kind in enumerate((DEP_X, DEP_Y, DEP_CORNER)):
                arrive(kind, s, dep_in.at[s, part])
            at_x, at_y, at_corner = [dep_in[s, part] for part in range(3)]
        else:
            for d in range(8):
                arrive(MAIL + d, s, mail_in.at[s, d, pl.ds(0, MAIL_TILES[d] * cells_y)])
            at_x, at_y, at_corner = tile(0, 0), tile(2, 0), tile(4, 0)

            def at_first(value):
                return jnp.where(first_row, value, 0.0)

            last_x = mail_in[s, 4, 2 * cells_y - 1 : 2 * cells_y, :]
            last_y = mail_in[s, 4, 3 * cells_y - 1 : 3 * cells_y, :]
            x_high = tile(1, 0) + kept[0] + at_first(tile(2, 2) + tile(7, 0))
            y_high = tile(3, 0) + kept[1] + at_first(tile(0, 2) + tile(6, 0))
            corner = tile(5, 0) + kept[2] + tile(1, 1) + tile(3, 1)
            halo[s + 1, X_HIGH] = jnp.where(inside(1, 0), x_high, 0.0)
            halo[s + 1, Y_HIGH] = jnp.where(inside(0, 1), y_high, 0.0)
            halo[s + 1, CORNER] = jnp.where(inside(1, 1), corner, 0.0)
            halo[s + 1, X_LOW] = tile(0, 1) + at_first(last_x)
            halo[s + 1, Y_LOW] = tile(2, 1) + at_first(last_y)
        for x in range(cells_x):
            extra = jnp.where(first_row, at_y[x : x + 1, :], 0.0)
            if x == 0:
                extra = extra + at_x + at_corner
            after[x] = partial[x] + extra

    for there, made in pending:

        @pl.when(there)
        def _():
            made.wait_send()


def local(
    slabs, bricks,
    pressure, previous, radius, velocity, positions, occupancy, anchors, migrations, crossings,
):
    cells_x, cells_y, depth = pressure.shape
    bins = radius.shape[0]
    most = bins // 2
    vmem = pl.BlockSpec(memory_space=pltpu.VMEM)
    hbm = pl.BlockSpec(memory_space=pltpu.HBM)
    scratch = [
        pltpu.VMEM(pressure.shape, F32),
        pltpu.VMEM(previous.shape, F32),
        pltpu.VMEM(radius.shape, F32),
        pltpu.VMEM(velocity.shape, F32),
        pltpu.VMEM(positions.shape, F32),
        pltpu.VMEM((1, bins), jnp.int32),
        pltpu.VMEM(anchors.shape, jnp.int32),
        pltpu.VMEM(migrations.shape, jnp.int32),
        pltpu.VMEM((1, STEPS), jnp.int32),
        pltpu.VMEM((STEPS, 5, cells_y, depth), F32),
        pltpu.VMEM((STEPS, 2, cells_y, depth), F32),
        pltpu.VMEM((STEPS, 3, cells_y, depth), F32),
        pltpu.VMEM((STEPS, 3 * cells_y, depth), F32),
        pltpu.VMEM((STEPS, 2, most, 4 * BIN), F32),
        pltpu.VMEM((STEPS, bins, 4 * BIN), F32),
        pltpu.VMEM((STEPS, bins, 4 * BIN), F32),
        pltpu.VMEM((STEPS, 2, most, 2 * BIN), F32),
        pltpu.VMEM((STEPS, bins, 2 * BIN), F32),
        pltpu.VMEM((bins, 2 * BIN), F32),
        pltpu.VMEM((2, 8, 128), jnp.int32),
        pltpu.VMEM((STEPS - 1, cells_x, cells_y, depth), F32),
        pltpu.VMEM((4 * bins, depth), F32),
        pltpu.VMEM((4 * bins, depth), F32),
        pltpu.VMEM((bins, 2 * BIN), F32),
        pltpu.VMEM((STEPS, 4 * bins, BIN), jnp.int32),
        pltpu.VMEM((STEPS, 4 * bins, 128), BF16),
        pltpu.VMEM((STEPS, 128, 4 * bins), BF16),
        pltpu.VMEM((STEPS + 1, bins, bins), BF16),
        pltpu.VMEM((4 * bins, BIN), F32),
        pltpu.VMEM((4 * bins, BIN), F32),
        pltpu.VMEM((4, bins, BIN), F32),
        pltpu.VMEM((bins, BIN), F32),
        pltpu.VMEM((PZ * bins, BIN), BF16),
        pltpu.VMEM((PZ * bins, BIN), BF16),
        pltpu.VMEM((STEPS - 1, 8, 3 * cells_y, depth), F32),
        pltpu.VMEM((STEPS - 1, 8, 3 * cells_y, depth), F32),
        pltpu.VMEM(pressure.shape, F32),
        pltpu.VMEM((3, cells_y, depth), F32),
        pltpu.SemaphoreType.DMA((STEPS, KINDS)),
        pltpu.SemaphoreType.DMA((STEPS, KINDS)),
        pltpu.SemaphoreType.DMA((9,)),
    ]
    results = pl.pallas_call(
        functools.partial(kernel, slabs, bricks),
        out_shape=(
            jax.ShapeDtypeStruct(pressure.shape, F32),
            jax.ShapeDtypeStruct(radius.shape, F32),
            jax.ShapeDtypeStruct(velocity.shape, F32),
        ),
        in_specs=[hbm] * 9,
        out_specs=(vmem,) * 3,
        scratch_shapes=scratch,
        compiler_params=pltpu.CompilerParams(
            collective_id=0, has_side_effects=True, vmem_limit_bytes=60 * 1024 * 1024
        ),
    )(
        pressure, previous, radius, velocity, positions, occupancy.reshape(1, bins), anchors,
        migrations, crossings.reshape(1, STEPS),
    )
    return pl.pallas_call(
        handed_on,
        out_shape=tuple(jax.ShapeDtypeStruct(x.shape, F32) for x in results),
        in_specs=[hbm] * 3,
        out_specs=(hbm,) * 3,
        scratch_shapes=[pltpu.VMEM(x.shape, F32) for x in results]
        + [pltpu.SemaphoreType.DMA((2, 3))],
        compiler_params=pltpu.CompilerParams(vmem_limit_bytes=60 * 1024 * 1024),
    )(*results)


def handed_on(*refs):
    given, wanted, held, sem = refs[:3], refs[3:6], refs[6:9], refs[9]
    fetched = [pltpu.make_async_copy(given[i], held[i], sem.at[0, i]) for i in range(3)]
    stored = [pltpu.make_async_copy(held[i], wanted[i], sem.at[1, i]) for i in range(3)]
    for copy in fetched:
        copy.start()
    for i in range(3):
        fetched[i].wait()
        stored[i].start()
    for copy in stored:
        copy.wait()


def solution(mesh):
    placed = (
        P("slab", "brick", None),
        P("slab", "brick", None),
        P(("slab", "brick"), None),
        P(("slab", "brick"), None),
        P(None, ("slab", "brick"), None),
        P(("slab", "brick")),
        P(None, None, ("slab", "brick")),
        P(None, ("slab", "brick")),
        P(None, ("slab", "brick")),
    )
    return jax.shard_map(
        functools.partial(local, mesh.shape["slab"], mesh.shape["brick"]),
        mesh=mesh,
        in_specs=placed,
        out_specs=(
            P("slab", "brick", None),
            P(("slab", "brick"), None),
            P(("slab", "brick"), None),
        ),
        check_vma=False,
    )
```
